128 devices in a mesh: frame: 32 (over z, y_hi, x), head: 4 (over y_lo, core).
Axes of the slice: x: 4, y: 4 (y_hi: 2, y_lo: 2; y = y_hi * 2 + y_lo), z: 4, core: 2. Of those that a mesh axis runs over, the one named last changes fastest.
Arguments:
- queries: bfloat16 [24576, 3072], P('frame', 'head'), may hold values from -20 to 20
- keys: bfloat16 [24576, 3072], P('frame', 'head'), may hold values from -20 to 20
- values: bfloat16 [24576, 3072], P('frame', 'head'), may hold values from -6 to 6
- block_mask: int32 [192, 192], P('frame'), may hold values from 0 to 1, as said below
- out_weight: bfloat16 [3072, 3072], P('head'), may hold values from -0.4375 to 0.4375
Outputs:
- projected: bfloat16 [24576, 3072], P(('frame', 'head'))
The draws below stay inside these ranges and needn't reach their ends.
Inputs may be any that keep to these rules, and one draw needn't show every extreme that they name: `block_mask`: group g holds the blocks g * 6 to (g + 1) * 6 - 1. A query block attends to every key block of its own group. Toward a group at distance d = 1, 2, 4 or 8 it attends to exactly max(1, 768 // (128 * 2 * d)) key blocks of that group, cyclically consecutive from a drawn start; to groups at any other distance to none.
All inputs are finite; a program needn't handle non-finite values.
Results may differ from the reference program's by a relative error of at most 0.015.
Values may be sent and summed in bfloat16 or wider, within the bound.
A program may use at most 320 MiB of HBM per device.

```python
import jax
import jax.numpy as jnp
from jax import lax

D = 3072
HEADS = 24
HEAD_DIM = 128
BLK = 128
TOK_DEV = 768
TOKENS = 24576
NBLK = 192
N_FRAME = 32


def draw_queries(key, part):
    key = jax.random.fold_in(key, 11)
    result = 1.5 * jnp.clip(jax.random.normal(key, (TOKENS, HEADS * HEAD_DIM), jnp.float32), -4.0, 4.0)
    return result.astype(jnp.bfloat16)


def draw_keys(key, part):
    key = jax.random.fold_in(key, 23)
    result = 1.5 * jnp.clip(jax.random.normal(key, (TOKENS, HEADS * HEAD_DIM), jnp.float32), -4.0, 4.0)
    return result.astype(jnp.bfloat16)


def draw_block_mask(key, part):
    key = jax.random.fold_in(key, 37)
    per_group = TOK_DEV // BLK
    groups = NBLK // per_group
    query_block = jnp.arange(NBLK, dtype=jnp.int32)[:, None]
    key_block = jnp.arange(NBLK, dtype=jnp.int32)[None, :]
    distance = jnp.abs(key_block // per_group - query_block // per_group)
    within = key_block % per_group
    starts = jax.random.randint(key, (NBLK, groups), 0, per_group, jnp.int32)
    start = starts[:, jnp.arange(NBLK, dtype=jnp.int32) // per_group]
    count = jnp.maximum(1, per_group // (2 * jnp.maximum(distance, 1)))
    keep = (within - start) % per_group < count
    banded = (distance == 1) | (distance == 2) | (distance == 4) | (distance == 8)
    result = jnp.where(distance == 0, 1, jnp.where(banded & keep, 1, 0))
    return result.astype(jnp.int32)


def steps_of(rng, shape, cuts, low, top_value):
    def one(axis_at, shards_of):
        steps = jax.random.uniform(jax.random.fold_in(jax.random.fold_in(rng, 6), axis_at), (shards_of,), jnp.float32, low / len(cuts), top_value / len(cuts))
        return jnp.repeat(jnp.exp(steps), shape[axis_at] // shards_of).reshape((-1,) + (1,) * (len(shape) - axis_at - 1))

    factor_of = one(*cuts[0])
    for cut in cuts[1:]:
        factor_of = factor_of * one(*cut)
    return factor_of


def gaussian(key, extent, deviation, reach, pieces=(), kind=jnp.bfloat16):
    loudness = steps_of(key, extent, pieces, -0.22, 0.18) if pieces else 1.0
    array = jax.random.normal(key, extent, jnp.float32) * deviation * loudness
    return jnp.minimum(jnp.maximum(array, -reach), reach).astype(kind)


def setup_inputs(seed: int = 0) -> dict:
    seeds = jax.random.split(jax.random.key(seed), 6)
    queries = draw_queries(jax.random.fold_in(seeds[5], 71), 0)
    keys = draw_keys(jax.random.fold_in(seeds[5], 71), 0)
    values = gaussian(seeds[2], (TOKENS, HEADS * HEAD_DIM), 1.0, 6.0, ((0, 32), (1, 4)))
    block_mask = draw_block_mask(jax.random.fold_in(seeds[5], 71), 0)
    out_weight = gaussian(seeds[4], (HEADS * HEAD_DIM, D), (HEADS * HEAD_DIM // 16) ** -0.5, 0.4375, ((0, 4),))
    return dict(queries=queries, keys=keys, values=values, block_mask=block_mask, out_weight=out_weight)


def reference(queries, keys, values, block_mask, out_weight):
    per_group = TOK_DEV // BLK
    scale = HEAD_DIM ** -0.5
    shape4 = (N_FRAME, TOK_DEV, HEADS, HEAD_DIM)
    query_groups = queries.reshape(shape4)
    key_groups = keys.reshape(shape4)
    value_groups = values.reshape(shape4)
    offsets = [0] + [s for d in (1, 2, 4, 8) if d < N_FRAME for s in (d, -d)]

    def one_group(group):
        group_queries = lax.dynamic_index_in_dim(query_groups, group, 0, keepdims=False).astype(jnp.float32)
        row_mask = lax.dynamic_slice_in_dim(block_mask, (group * per_group).astype(jnp.int32), per_group, 0)
        key_list, value_list, live_list = [], [], []
        for offset in offsets:
            source = group - offset
            valid = (source >= 0) & (source < N_FRAME)
            clipped = jnp.clip(source, 0, N_FRAME - 1).astype(jnp.int32)
            key_list.append(lax.dynamic_index_in_dim(key_groups, clipped, 0, keepdims=False).astype(jnp.float32))
            value_list.append(lax.dynamic_index_in_dim(value_groups, clipped, 0, keepdims=False).astype(jnp.float32))
            columns = lax.dynamic_slice_in_dim(row_mask, (clipped * per_group).astype(jnp.int32), per_group, 1)
            live = (columns > 0) & valid
            live_tokens = jnp.broadcast_to(live[:, None, :, None], (per_group, BLK, per_group, BLK)).reshape(TOK_DEV, TOK_DEV)
            live_list.append(live_tokens)
        all_keys = jnp.concatenate(key_list, axis=0)
        all_values = jnp.concatenate(value_list, axis=0)
        all_live = jnp.concatenate(live_list, axis=1)

        def one_head(head):
            head_queries = lax.dynamic_index_in_dim(group_queries, head, 1, keepdims=False)
            head_keys = lax.dynamic_index_in_dim(all_keys, head, 1, keepdims=False)
            head_values = lax.dynamic_index_in_dim(all_values, head, 1, keepdims=False)
            scores = jnp.dot(head_queries, head_keys.T) * scale
            scores = jnp.where(all_live, scores, -jnp.inf)
            top = jnp.max(scores, axis=1, keepdims=True)
            probs = jnp.exp(scores - top)
            total = jnp.sum(probs, axis=1, keepdims=True)
            rounded = lax.optimization_barrier(probs.astype(jnp.bfloat16))
            return jnp.dot(rounded.astype(jnp.float32), head_values) / total

        heads_out = lax.map(one_head, jnp.arange(HEADS, dtype=jnp.int32))
        return jnp.transpose(heads_out, (1, 0, 2)).reshape(TOK_DEV, HEADS * HEAD_DIM).astype(jnp.bfloat16)

    attended = lax.map(one_group, jnp.arange(N_FRAME, dtype=jnp.int32)).reshape(TOKENS, HEADS * HEAD_DIM)
    return jnp.dot(attended, out_weight, preferred_element_type=jnp.float32).astype(jnp.bfloat16)
```

```python
import math

import jax
import jax.numpy as jnp
from jax import lax
from jax.experimental import pallas as pl
from jax.experimental.pallas import tpu as pltpu
from jax.sharding import PartitionSpec as P

HEAD_DIM = 128
BLK = 128
GROUP = 768
PER_GROUP = GROUP // BLK
WIDTH = 3072
HEADS_CHIP = 12
PLANE = 8
CHUNK = 512
CHUNKS = WIDTH // CHUNK
DISTANCES = (1, 2, 4, 8)
EXP2_SCALE = HEAD_DIM ** (-0.5) * math.log2(math.e)
NEG = -1e30
MESH = pl.DeviceIdType.MESH


def live_blocks(block_mask):
    me = lax.axis_index("frame")
    groups = lax.axis_size("frame")
    mask = block_mask.reshape(PER_GROUP, groups, PER_GROUP)
    begins = (mask > 0) & (jnp.roll(mask, 1, axis=2) == 0)
    first = jnp.sum(jnp.where(begins, jnp.arange(PER_GROUP, dtype=jnp.int32), 0), axis=2)
    offsets = jnp.array([s * d for d in DISTANCES for s in (-1, 1)], jnp.int32)
    wanted = jnp.arange(groups, dtype=jnp.int32)[:, None] == (me + offsets)[None, :]
    starts = jnp.sum(jnp.where(wanted[None], first[:, :, None], 0), axis=1)
    nearest = (starts[:, :2, None] + jnp.arange(3, dtype=jnp.int32)) % PER_GROUP
    blocks = jnp.concatenate([nearest.reshape(PER_GROUP, 6), starts[:, 2:]], axis=1)
    return jnp.zeros((8, 128), jnp.int32).at[:PER_GROUP, :12].set(blocks)


def kernel(
    q_hbm, k_hbm, v_hbm, blocks_ref, w_hbm, out_ref,
    plane, zbuf, qbuf, idx_v, idx_s, wbuf, acc, top_s, sum_s, obuf, att, sbuf, rbuf, own,
    kv_ss, q_ss, i_ss, pf_ss, z_ss, zf_ss, w_ss, o_ss, r_ss,
    p_rs, pf_rs, q_rs, i_rs, z_rs, zf_rs, w_rs, w_ls, a_rs, r_rs, s_sem,
):
    f = lax.axis_index("frame")
    h = lax.axis_index("head")
    z, yh, x = f // 8, lax.rem(f // 4, 2), lax.rem(f, 4)
    yl, c = h // 2, lax.rem(h, 2)
    g_me = lax.rem(f, 8)
    has_low, has_high = z > 0, z < 3

    def device(z_, g_, yl_, c_):
        return {"frame": z_ * 8 + g_, "head": yl_ * 2 + c_}

    other_core = device(z, g_me, yl, 1 - c)

    def remote(src, dst, ss, rs, target):
        return pltpu.make_async_remote_copy(
            src_ref=src, dst_ref=dst, send_sem=ss, recv_sem=rs, device_id=target, device_id_type=MESH
        )

    def is_me(target):
        return (target["frame"] == f) & (target["head"] == h)

    def send_or_copy(src, dst, ss, rs, target):
        mine = is_me(target)

        @pl.when(jnp.logical_not(mine))
        def _():
            remote(src, dst, ss, rs, target).start()

        @pl.when(mine)
        def _():
            pltpu.make_async_copy(src, dst, rs).start()

    def sent(src, dst, ss, rs, target):
        @pl.when(jnp.logical_not(is_me(target)))
        def _():
            remote(src, dst, ss, rs, target).wait_send()

    def arrived(ref, sem):
        pltpu.make_async_copy(ref, ref, sem).wait()

    barrier = pltpu.get_barrier_semaphore()

    def greet(target):
        pl.semaphore_signal(barrier, inc=1, device_id=target, device_id_type=MESH)

    def greet_plane(i, carry):
        target = device(z, i // 2, yl, lax.rem(i, 2))

        @pl.when(jnp.logical_not(is_me(target)))
        def _():
            greet(target)

        return carry

    lax.fori_loop(0, 2 * PLANE, greet_plane, 0)
    partner = [device(z, g_me, 1 - yl, c), device(z, (1 - yh) * 4 + x, 1 - yl, c)]
    for target in partner:
        greet(target)
    low, high = device(z - 1, g_me, yl, c), device(z + 1, g_me, yl, c)

    @pl.when(has_low)
    def _():
        greet(low)

    @pl.when(has_high)
    def _():
        greet(high)

    pl.semaphore_wait(barrier, 17 + has_low.astype(jnp.int32) + has_high.astype(jnp.int32))

    e_me = x + yh * (3 - 2 * x)

    def idx_copies():
        for i in range(2):
            for j in range(2):
                yield (blocks_ref, idx_v.at[e_me], i_ss.at[i, j], i_rs.at[e_me],
                       device(z, j * 4 + 2 * c + i, yl, yh))

    def kv_copies():
        for n, (j, to) in enumerate(((0, 0), (1, 1), (2, 0), (2, 1))):
            for i in range(2):
                for t, src in enumerate((k_hbm, v_hbm)):
                    hs = j // 2
                    yield (src.at[:, :, pl.ds((3 * i + j) * HEAD_DIM, HEAD_DIM)], plane.at[t, hs, g_me],
                           kv_ss.at[t, i, n], p_rs.at[hs, g_me], device(z, to * 4 + 2 * c + i, yl, t))

    def q_copies():
        for i in range(2):
            for j in range(3):
                to, slot = (j, e_me) if j < 2 else (e_me // 2, 4 + lax.rem(e_me, 2))
                yield (q_hbm.at[:, :, pl.ds((3 * i + j) * HEAD_DIM, HEAD_DIM)], qbuf.at[slot],
                       q_ss.at[i, j], q_rs.at[slot], device(z, to * 4 + 2 * c + i, yl, yh))

    for args in idx_copies():
        send_or_copy(*args)
    for args in kv_copies():
        send_or_copy(*args)
    for args in q_copies():
        send_or_copy(*args)
    w_local = pltpu.make_async_copy(w_hbm, wbuf.at[c], w_ls)
    w_remote = remote(w_hbm, wbuf.at[c], w_ss, w_rs, other_core)
    w_local.start()

    def piece(step):
        hs = step // PLANE
        g = lax.bitwise_xor(lax.rem(step, PLANE), g_me)
        return hs, g

    def to_high(hs, g):
        return (hs == 0) | (g // 2 != 1 - yh)

    def to_low(hs, g):
        return (hs == 0) | (g // 2 != 2 + yh)

    def z_copy(way, hs, g):
        return remote(plane.at[c, hs, g], zbuf.at[way, c, hs, g], z_ss.at[way, hs, g], z_rs.at[way, hs, g],
                      (high, low)[way])

    def plane_forward(hs, g):
        return remote(plane.at[c, hs, g], plane.at[c, hs, g], pf_ss.at[hs, g], pf_rs.at[hs, g], other_core)

    def z_forward(way, hs, g):
        return remote(zbuf.at[way, c, hs, g], zbuf.at[way, c, hs, g], zf_ss.at[way, hs, g], zf_rs.at[way, hs, g],
                      other_core)

    def spread(step, carry):
        hs, g = piece(step)
        arrived(plane.at[c, hs, g], p_rs.at[hs, g])

        @pl.when(has_high & to_high(hs, g))
        def _():
            z_copy(0, hs, g).start()

        @pl.when(has_low & to_low(hs, g))
        def _():
            z_copy(1, hs, g).start()

        plane_forward(hs, g).start()
        return carry

    def gets(way, hs, g):
        return (has_low & to_high(hs, g), has_high & to_low(hs, g))[way]

    def pass_on(step, carry):
        hs, g = piece(step)
        for way in range(2):

            @pl.when(gets(way, hs, g))
            def _():
                arrived(zbuf.at[way, c, hs, g], z_rs.at[way, hs, g])
                z_forward(way, hs, g).start()

        return carry

    lax.fori_loop(0, 2 * PLANE, spread, 0)
    w_remote.start()
    lax.fori_loop(0, 8, pass_on, 0)

    def other_plane(step, carry):
        hs, g = piece(step)
        arrived(plane.at[1 - c, hs, g], pf_rs.at[hs, g])
        return carry

    lax.fori_loop(0, 2 * PLANE, other_plane, 0)
    for e in range(4):
        arrived(idx_v.at[e], i_rs.at[e])
    load_idx = pltpu.make_async_copy(idx_v, idx_s, s_sem)
    load_idx.start()
    load_idx.wait()
    for u in range(6):
        arrived(qbuf.at[u], q_rs.at[u])

    def frame_at(e):
        return e + c * (7 - 2 * e)

    def scores_of(q, keys):
        return lax.dot_general(q, keys, (((1,), (1,)), ((), ())), preferred_element_type=jnp.float32)

    def rows_at(qb):
        return pl.ds(pl.multiple_of(qb * BLK, BLK), BLK)

    def block(e, qb, d, way, j=0):
        return idx_s[e, qb, 3 * way + j if d == 0 else 4 + 2 * d + way]

    def plane_part(u, e, hs, out1, out2, qb):
        g = frame_at(e)
        near = [(frame_at(e + 1), block(e, qb, 0, 1 - c, j)) for j in range(3)]
        near += [(frame_at(e + 2), block(e, qb, 1, 1 - c)), (frame_at(e + 4), block(e, qb, 2, 1 - c))]
        if out1:
            near += [(frame_at(e - 1), block(e, qb, 0, c, j)) for j in range(3)]
        if out2:
            near += [(frame_at(e - 2), block(e, qb, 1, c))]
        q = qbuf[u, qb]

        def taken(t):
            return jnp.concatenate(
                [plane[t, hs, g].reshape(GROUP, HEAD_DIM)] + [plane[t, hs, gg, b] for gg, b in near], axis=0
            )

        keys, vals = taken(0), taken(1)
        s = scores_of(q, keys)
        top = jnp.max(s, axis=1, keepdims=True)
        p = jnp.exp2((s - top) * EXP2_SCALE)
        total = jnp.sum(p, axis=1, keepdims=True)
        acc[u, rows_at(qb), :] = jnp.dot(p.astype(jnp.bfloat16), vals, preferred_element_type=jnp.float32)
        top_s[u, rows_at(qb), :] = jnp.broadcast_to(top, (BLK, HEAD_DIM))
        sum_s[u, rows_at(qb), :] = jnp.broadcast_to(total, (BLK, HEAD_DIM))

    def z_part(u, e, hs, out1, out2, qb):
        g = frame_at(e)
        far = [(0, g, block(e, qb, 3, 0)), (1, g, block(e, qb, 3, 1)), (c, frame_at(e + 4), block(e, qb, 2, c))]
        if not out2:
            far += [(c, frame_at(e + 6), block(e, qb, 1, c))]
        if not out1:
            far += [(c, frame_at(e + 7), block(e, qb, 0, c, j)) for j in range(3)]
        q = qbuf[u, qb]
        keys, vals, valid = [], [], []
        for way, gg, b in far:
            ok = ((way == 0) & has_low) | ((way == 1) & has_high)
            w2 = jnp.where(ok, way, 1 - way)
            g2 = jnp.where(ok, gg, g)
            keys.append(zbuf[w2, 0, hs, g2, b])
            vals.append(zbuf[w2, 1, hs, g2, b])
            valid.append(jnp.where(ok, 0.0, NEG))
        s = scores_of(q, jnp.concatenate(keys, axis=0))
        s = jnp.concatenate(
            [s[:, n * BLK : (n + 1) * BLK] + valid[n] for n in range(len(far))], axis=1
        )
        old = top_s[u, rows_at(qb), :]
        top = jnp.maximum(old[:, :1], jnp.max(s, axis=1, keepdims=True))
        p = jnp.exp2((s - top) * EXP2_SCALE)
        keep = jnp.exp2((old - top) * EXP2_SCALE)
        total = sum_s[u, rows_at(qb), :] * keep + jnp.sum(p, axis=1, keepdims=True)
        o = acc[u, rows_at(qb), :] * keep + jnp.dot(
            p.astype(jnp.bfloat16), jnp.concatenate(vals, axis=0), preferred_element_type=jnp.float32
        )
        obuf[u, rows_at(qb), :] = (o / total).astype(jnp.bfloat16)

    kinds = (
        (2 - yh, lambda n: (4 * n, 0, n), False, False),
        (2 - yh, lambda n: (1 + 4 * n, 1, n), True, False),
        (2 + 2 * yh, lambda n: (2 + n, 2 + lax.rem(n, 2), n // 2), True, True),
    )
    for step, (count, unit, out1, out2) in enumerate(kinds):

        def plane_unit(n, carry, unit=unit, out1=out1, out2=out2):
            u, e, hs = unit(n)

            def one(qb, carry2):
                plane_part(u, e, hs, out1, out2, qb)
                return carry2

            return lax.fori_loop(0, PER_GROUP, one, carry)

        lax.fori_loop(0, count, plane_unit, 0)
        lax.fori_loop(8 + 2 * step, 10 + 2 * step, pass_on, 0)
    lax.fori_loop(14, 16, pass_on, 0)

    def other_z(step, carry):
        hs, g = piece(step)
        for way in range(2):

            @pl.when(gets(way, hs, g))
            def _():
                arrived(zbuf.at[way, 1 - c, hs, g], zf_rs.at[way, hs, g])

        return carry

    lax.fori_loop(0, 2 * PLANE, other_z, 0)

    def o_copies(u, e, hs):
        head = 3 * x + jnp.where(hs == 0, yh, 2)
        cols = pl.ds(pl.multiple_of(head * HEAD_DIM, HEAD_DIM), HEAD_DIM)
        x_to = e + c * (3 - 2 * e)
        here, across = c * 4 + x_to, (1 - c) * 4 + x_to
        for t in range(2):
            mine, theirs = (2 * yl + t) * 192, (2 * (1 - yl) + t) * 192
            parts = ((mine, 192, 192, here), (theirs, 96, 0, here), (theirs + 96, 96, 96, across))
            for k, (row, size, at, to) in enumerate(parts):
                yield (obuf.at[u, pl.ds(pl.multiple_of(row, 96), size), :], att.at[pl.ds(at, size), cols],
                       o_ss.at[u, t, k], a_rs.at[k], device(z, to, yl, t))

    for count, unit, out1, out2 in kinds:

        def z_unit(n, carry, unit=unit, out1=out1, out2=out2):
            u, e, hs = unit(n)

            def one(qb, carry2):
                z_part(u, e, hs, out1, out2, qb)
                return carry2

            lax.fori_loop(0, PER_GROUP, one, 0)
            for args in o_copies(u, e, hs):
                send_or_copy(*args)
            return carry

        lax.fori_loop(0, count, z_unit, 0)

    w_local.wait()
    arrived(wbuf.at[1 - c], w_rs)
    arrived(att.at[pl.ds(192, 192)], a_rs.at[0])
    arrived(att.at[pl.ds(0, 96)], a_rs.at[1])
    arrived(att.at[pl.ds(96, 96)], a_rs.at[2])

    def r_copy(n, k):
        cols = pl.ds(pl.multiple_of(n * CHUNK, CHUNK), CHUNK)
        rows = pl.ds(96 * k, 96)
        return remote(sbuf.at[rows, cols], rbuf.at[rows, cols], r_ss.at[n, k], r_rs.at[n, k], partner[k])

    half = HEADS_CHIP // 2 * HEAD_DIM

    def project(n, carry):
        cols = pl.ds(pl.multiple_of(n * CHUNK, CHUNK), CHUNK)
        r = jnp.dot(att[:, :half], wbuf[0, :, cols], preferred_element_type=jnp.float32)
        r = r + jnp.dot(att[:, half:], wbuf[1, :, cols], preferred_element_type=jnp.float32)
        sbuf[:, cols] = r[:192].astype(jnp.bfloat16)
        own[:, cols] = r[192:]
        for k in range(2):
            r_copy(n, k).start()
        return carry

    lax.fori_loop(0, CHUNKS, project, 0)

    def finish(n, carry):
        cols = pl.ds(pl.multiple_of(n * CHUNK, CHUNK), CHUNK)
        for k in range(2):
            r_copy(n, k).wait()
        out_ref[:, cols] = (own[:, cols] + rbuf[:, cols].astype(jnp.float32)).astype(jnp.bfloat16)
        return carry

    lax.fori_loop(0, CHUNKS, finish, 0)

    for copies in (idx_copies, kv_copies, q_copies):
        for args in copies():
            sent(*args)
    w_remote.wait_send()

    def done(step, carry):
        hs, g = piece(step)
        plane_forward(hs, g).wait_send()

        @pl.when(has_high & to_high(hs, g))
        def _():
            z_copy(0, hs, g).wait_send()

        @pl.when(has_low & to_low(hs, g))
        def _():
            z_copy(1, hs, g).wait_send()

        for way in range(2):

            @pl.when(gets(way, hs, g))
            def _():
                z_forward(way, hs, g).wait_send()

        return carry

    lax.fori_loop(0, 2 * PLANE, done, 0)
    for count, unit, out1, out2 in kinds:

        def o_done(n, carry, unit=unit):
            for args in o_copies(*unit(n)):
                sent(*args)
            return carry

        lax.fori_loop(0, count, o_done, 0)


def per_device(queries, keys, values, block_mask, out_weight):
    blocks = live_blocks(block_mask)
    dma = pltpu.SemaphoreType.DMA
    bf16, f32 = jnp.bfloat16, jnp.float32
    rows, piece = (GROUP, HEAD_DIM), (PER_GROUP, BLK, HEAD_DIM)
    scratch = [
        pltpu.VMEM((2, 2, PLANE, *piece), bf16),
        pltpu.VMEM((2, 2, 2, PLANE, *piece), bf16),
        pltpu.VMEM((6, *piece), bf16),
        pltpu.VMEM((4, 8, 128), jnp.int32),
        pltpu.SMEM((4, 8, 128), jnp.int32),
        pltpu.VMEM((2, *out_weight.shape), bf16),
        pltpu.VMEM((6, *rows), f32),
        pltpu.VMEM((6, *rows), f32),
        pltpu.VMEM((6, *rows), f32),
        pltpu.VMEM((6, *rows), bf16),
        pltpu.VMEM((384, HEADS_CHIP * HEAD_DIM), bf16),
        pltpu.VMEM((192, WIDTH), bf16),
        pltpu.VMEM((192, WIDTH), bf16),
        pltpu.VMEM((192, WIDTH), f32),
        dma((2, 2, 4)), dma((2, 3)), dma((2, 2)), dma((2, 8)), dma((2, 2, 8)), dma((2, 2, 8)), dma, dma((6, 2, 3)),
        dma((CHUNKS, 2)),
        dma((2, 8)), dma((2, 8)), dma((6,)), dma((4,)), dma((2, 2, 8)), dma((2, 2, 8)), dma, dma, dma((3,)),
        dma((CHUNKS, 2)), dma,
    ]
    any_space = pl.BlockSpec(memory_space=pl.ANY)
    vmem = pl.BlockSpec(memory_space=pltpu.VMEM)
    return pl.pallas_call(
        kernel,
        out_shape=jax.ShapeDtypeStruct((192, WIDTH), bf16),
        in_specs=[any_space, any_space, any_space, vmem, any_space],
        out_specs=vmem,
        scratch_shapes=scratch,
        compiler_params=pltpu.CompilerParams(
            collective_id=0, has_side_effects=True, vmem_limit_bytes=60 * 2**20
        ),
        name="attention",
    )(*(a.reshape(PER_GROUP, BLK, GROUP) for a in (queries, keys, values)), blocks, out_weight)


def solution(mesh):
    in_specs = (
        P("frame", "head"),
        P("frame", "head"),
        P("frame", "head"),
        P("frame", None),
        P("head", None),
    )
    out_specs = P(("frame", "head"), None)
    return jax.shard_map(
        per_device, mesh=mesh, in_specs=in_specs, out_specs=out_specs, check_vma=False
    )
```

```python
import math

import jax
import jax.numpy as jnp
from jax import lax
from jax.experimental import pallas as pl
from jax.experimental.pallas import tpu as pltpu
from jax.sharding import PartitionSpec as P

HEAD_DIM = 128
BLK = 128
GROUP = 768
PER_GROUP = GROUP // BLK
WIDTH = 3072
HEADS_CHIP = 12
PLANE = 8
CHUNK = 512
CHUNKS = WIDTH // CHUNK
EXP2_SCALE = HEAD_DIM ** (-0.5) * math.log2(math.e)
NEG = -1e30
MESH = pl.DeviceIdType.MESH


def live_blocks(mask):
    lane = lax.broadcasted_iota(jnp.int32, mask.shape, 1)
    at = lax.rem(lane, PER_GROUP)
    lanes = mask.shape[1]

    def ahead(value, by):
        return pltpu.roll(value, (lanes - by) % lanes, 1)

    before = jnp.where(at == 0, ahead(mask, PER_GROUP - 1), ahead(mask, lanes - 1))
    first = jnp.where((mask > 0) & (before == 0), at, 0)
    total = first
    for n in range(1, PER_GROUP):
        total = total + ahead(first, n)
    total = jnp.where((at == 0) & (lane < lanes - PER_GROUP), total, 0)
    shared = total
    for n in range(1, PER_GROUP):
        shared = shared + ahead(total, lanes - n)
    return lax.rem(shared + at, PER_GROUP)


def kernel(
    q_hbm, k_hbm, v_hbm, mask_ref, w_hbm, out_ref,
    plane_a, plane_c, z_a, z_c, qbuf, blocks_ref, idx_v, idx_s, w_a, w_c, acc, top_s, sum_s, obuf, att_a, att_c,
    sums, sbuf, rbuf,
    kv_ss, q_ss, i_ss, pf_ss, z_ss, zf_ss, w_ss, o_ss, r_ss,
    p_rs, pf_rs, q_rs, i_rs, z_rs, zf_rs, w_rs, w_ls, a_rs, r_rs, s_sem,
):
    plane, zbuf, att, wbuf = (plane_a, plane_c), (z_a, z_c), (att_a, att_c), (w_a, w_c)
    f = lax.axis_index("frame")
    h = lax.axis_index("head")
    z, yh, x = f // 8, lax.rem(f // 4, 2), lax.rem(f, 4)
    yl, c = h // 2, lax.rem(h, 2)
    g_me = lax.rem(f, 8)
    has_low, has_high = z > 0, z < 3

    def device(z_, g_, yl_, c_):
        return {"frame": z_ * 8 + g_, "head": yl_ * 2 + c_}

    other_core = device(z, g_me, yl, 1 - c)

    def remote(src, dst, ss, rs, target):
        return pltpu.make_async_remote_copy(
            src_ref=src, dst_ref=dst, send_sem=ss, recv_sem=rs, device_id=target, device_id_type=MESH
        )

    def is_me(target):
        return (target["frame"] == f) & (target["head"] == h)

    def send_or_copy(src, dst, ss, rs, target):
        mine = is_me(target)

        @pl.when(jnp.logical_not(mine))
        def _():
            remote(src, dst, ss, rs, target).start()

        @pl.when(mine)
        def _():
            pltpu.make_async_copy(src, dst, rs).start()

    def sent(src, dst, ss, rs, target):
        @pl.when(jnp.logical_not(is_me(target)))
        def _():
            remote(src, dst, ss, rs, target).wait_send()

    def arrived(ref, sem):
        pltpu.make_async_copy(ref, ref, sem).wait()

    barrier = pltpu.get_barrier_semaphore()

    def greet(target):
        pl.semaphore_signal(barrier, inc=1, device_id=target, device_id_type=MESH)

    def greet_plane(i, carry):
        target = device(z, i // 2, yl, lax.rem(i, 2))

        @pl.when(jnp.logical_not(is_me(target)))
        def _():
            greet(target)

        return carry

    lax.fori_loop(0, 2 * PLANE, greet_plane, 0)
    partner = [device(z, g_me, 1 - yl, c), device(z, (1 - yh) * 4 + x, 1 - yl, c)]
    for target in partner:
        greet(target)
    low, high = device(z - 1, g_me, yl, c), device(z + 1, g_me, yl, c)

    @pl.when(has_low)
    def _():
        greet(low)

    @pl.when(has_high)
    def _():
        greet(high)

    blocks_ref[...] = jnp.zeros_like(blocks_ref)
    blocks_ref[:PER_GROUP, : mask_ref.shape[1]] = mask_ref[...]
    blocks_ref[...] = live_blocks(blocks_ref[...])
    pl.semaphore_wait(barrier, 17 + has_low.astype(jnp.int32) + has_high.astype(jnp.int32))

    e_me = x + yh * (3 - 2 * x)

    def idx_copies():
        for i in range(2):
            for j in range(2):
                yield (blocks_ref, idx_v.at[e_me], i_ss.at[i, j], i_rs.at[e_me],
                       device(z, j * 4 + 2 * c + i, yl, yh))

    def kv_copies(hs):
        for n, (j, to) in (((0, (0, 0)), (1, (1, 1))), ((2, (2, 0)), (3, (2, 1))))[hs]:
            for i in range(2):
                for t, src in enumerate((k_hbm, v_hbm)):
                    yield (src.at[:, :, pl.ds((3 * i + j) * HEAD_DIM, HEAD_DIM)], plane[hs].at[t, g_me],
                           kv_ss.at[t, i, n], p_rs.at[hs, g_me], device(z, to * 4 + 2 * c + i, yl, t))

    def q_copies(hs):
        for i in range(2):
            for j in ((0, 1), (2,))[hs]:
                to, slot = (j, e_me) if j < 2 else (e_me // 2, 4 + lax.rem(e_me, 2))
                yield (q_hbm.at[:, :, pl.ds((3 * i + j) * HEAD_DIM, HEAD_DIM)], qbuf.at[slot],
                       q_ss.at[i, j], q_rs.at[slot], device(z, to * 4 + 2 * c + i, yl, yh))

    dealt = (lambda: kv_copies(0), idx_copies, lambda: q_copies(0), lambda: kv_copies(1), lambda: q_copies(1))
    for copies in dealt:
        for args in copies():
            send_or_copy(*args)

    def w_copies():
        for i in range(2):
            for hs, size in enumerate((256, 128)):
                yield (w_hbm.at[pl.ds(384 * i + 256 * hs, size), :],
                       wbuf[hs].at[pl.ds(pl.multiple_of((2 * c + i) * size, size), size), :], i, hs)

    for src, dst, i, hs in w_copies():
        pltpu.make_async_copy(src, dst, w_ls.at[i, hs]).start()

    def frame_of(step):
        return lax.bitwise_xor(step, g_me)

    def to_high(hs, g):
        return (g // 2 != 1 - yh) if hs else (g >= 0)

    def to_low(hs, g):
        return (g // 2 != 2 + yh) if hs else (g >= 0)

    def z_copy(way, hs, g):
        return remote(plane[hs].at[c, g], zbuf[hs].at[way, c, g], z_ss.at[way, hs, g], z_rs.at[way, hs, g],
                      (high, low)[way])

    def plane_forward(hs, g):
        return remote(plane[hs].at[c, g], plane[hs].at[c, g], pf_ss.at[hs, g], pf_rs.at[hs, g], other_core)

    def z_forward(way, hs, g):
        return remote(zbuf[hs].at[way, c, g], zbuf[hs].at[way, c, g], zf_ss.at[way, hs, g], zf_rs.at[way, hs, g],
                      other_core)

    def spread(hs, first, last):
        def one(step, carry):
            g = frame_of(step)
            arrived(plane[hs].at[c, g], p_rs.at[hs, g])

            @pl.when(has_high & to_high(hs, g))
            def _():
                z_copy(0, hs, g).start()

            @pl.when(has_low & to_low(hs, g))
            def _():
                z_copy(1, hs, g).start()

            plane_forward(hs, g).start()
            return carry

        lax.fori_loop(first, last, one, 0)

    def gets(way, hs, g):
        return (has_low & to_high(hs, g), has_high & to_low(hs, g))[way]

    def pass_on(hs, first, last):
        def one(step, carry):
            g = frame_of(step)
            for way in range(2):

                @pl.when(gets(way, hs, g))
                def _():
                    arrived(zbuf[hs].at[way, c, g], z_rs.at[way, hs, g])
                    z_forward(way, hs, g).start()

            return carry

        lax.fori_loop(first, last, one, 0)

    def other_plane(hs):
        def one(g, carry):
            arrived(plane[hs].at[1 - c, g], pf_rs.at[hs, g])
            return carry

        lax.fori_loop(0, PLANE, one, 0)

    def other_z(hs):
        def one(g, carry):
            for way in range(2):

                @pl.when(gets(way, hs, g))
                def _():
                    arrived(zbuf[hs].at[way, 1 - c, g], zf_rs.at[way, hs, g])

            return carry

        lax.fori_loop(0, PLANE, one, 0)

    def frame_at(e):
        return e + c * (7 - 2 * e)

    def scores_of(q, keys):
        return lax.dot_general(q, keys, (((1,), (1,)), ((), ())), preferred_element_type=jnp.float32)

    def rows_at(qb):
        return pl.ds(pl.multiple_of(qb * BLK, BLK), BLK)

    def block(e, qb, distance, way, j=0):
        group = z * PLANE + frame_at(e) + (2 * way - 1) * distance
        group = jnp.clip(group, 0, 4 * PLANE - 1)
        return idx_s[e, qb, group * PER_GROUP + j]

    def plane_part(u, e, hs, out1, out2, qb):
        g = frame_at(e)
        near = [(frame_at(e + 1), block(e, qb, 1, 1 - c, j)) for j in range(3)]
        near += [(frame_at(e + 2), block(e, qb, 2, 1 - c)), (frame_at(e + 4), block(e, qb, 4, 1 - c))]
        if out1:
            near += [(frame_at(e - 1), block(e, qb, 1, c, j)) for j in range(3)]
        if out2:
            near += [(frame_at(e - 2), block(e, qb, 2, c))]
        q = qbuf[u, qb]

        def taken(t):
            return jnp.concatenate(
                [plane[hs][t, g].reshape(GROUP, HEAD_DIM)] + [plane[hs][t, gg, b] for gg, b in near], axis=0
            )

        keys, vals = taken(0), taken(1)
        s = scores_of(q, keys)
        top = jnp.max(s, axis=1, keepdims=True)
        p = jnp.exp2((s - top) * EXP2_SCALE)
        total = jnp.sum(p, axis=1, keepdims=True)
        acc[u, rows_at(qb), :] = jnp.dot(p.astype(jnp.bfloat16), vals, preferred_element_type=jnp.float32)
        top_s[u, rows_at(qb), :] = jnp.broadcast_to(top, (BLK, HEAD_DIM))
        sum_s[u, rows_at(qb), :] = jnp.broadcast_to(total, (BLK, HEAD_DIM))

    def z_part(u, e, hs, out1, out2, qb):
        g = frame_at(e)
        far = [(0, g, block(e, qb, 8, 0)), (1, g, block(e, qb, 8, 1)), (c, frame_at(e + 4), block(e, qb, 4, c))]
        if not out2:
            far += [(c, frame_at(e + 6), block(e, qb, 2, c))]
        if not out1:
            far += [(c, frame_at(e + 7), block(e, qb, 1, c, j)) for j in range(3)]
        q = qbuf[u, qb]
        keys, vals, valid = [], [], []
        for way, gg, b in far:
            ok = ((way == 0) & has_low) | ((way == 1) & has_high)
            w2 = jnp.where(ok, way, 1 - way)
            g2 = jnp.where(ok, gg, g)
            keys.append(zbuf[hs][w2, 0, g2, b])
            vals.append(zbuf[hs][w2, 1, g2, b])
            valid.append(jnp.where(ok, 0.0, NEG))
        s = scores_of(q, jnp.concatenate(keys, axis=0))
        s = jnp.concatenate(
            [s[:, n * BLK : (n + 1) * BLK] + valid[n] for n in range(len(far))], axis=1
        )
        old = top_s[u, rows_at(qb), :]
        top = jnp.maximum(old[:, :1], jnp.max(s, axis=1, keepdims=True))
        p = jnp.exp2((s - top) * EXP2_SCALE)
        keep = jnp.exp2((old - top) * EXP2_SCALE)
        total = sum_s[u, rows_at(qb), :] * keep + jnp.sum(p, axis=1, keepdims=True)
        o = acc[u, rows_at(qb), :] * keep + jnp.dot(
            p.astype(jnp.bfloat16), jnp.concatenate(vals, axis=0), preferred_element_type=jnp.float32
        )
        obuf[u, rows_at(qb), :] = (o / total).astype(jnp.bfloat16)

    def query_blocks(first, last, unroll, part, *unit):
        def one(qb, carry):
            part(*unit, first + qb)
            return carry

        lax.fori_loop(0, last, one, 0, unroll=unroll)

    def o_copies(u, e, hs, ks):
        head = x if hs else 2 * x + yh
        cols = pl.ds(pl.multiple_of(head * HEAD_DIM, HEAD_DIM), HEAD_DIM)
        x_to = e + c * (3 - 2 * e)
        here, across = c * 4 + x_to, (1 - c) * 4 + x_to
        for t in range(2):
            mine, theirs = (2 * yl + t) * 192, (2 * (1 - yl) + t) * 192
            parts = ((mine, 192, 192, here), (theirs, 96, 0, here), (theirs + 96, 96, 96, across))
            for k in ks:
                row, size, at, to = parts[k]
                yield (obuf.at[u, pl.ds(pl.multiple_of(row, 96), size), :], att[hs].at[pl.ds(at, size), cols],
                       o_ss.at[u, t, k], a_rs.at[hs, k], device(z, to, yl, t))

    def att_arrived(hs, ks):
        for k in ks:
            row, size = ((192, 192), (0, 96), (96, 96))[k]
            arrived(att[hs].at[pl.ds(row, size)], a_rs.at[hs, k])

    own_kinds = (
        (1, lambda n: (0, 0), False, False),
        (1, lambda n: (1, 1), True, False),
        (2, lambda n: (2 + n, 2 + n), True, True),
    )
    shared_kinds = (
        (1 - yh, lambda n: (4, 0), False, False),
        (1 - yh, lambda n: (5, 1), True, False),
        (2 * yh, lambda n: (4 + n, 2 + n), True, True),
    )

    spread(0, 0, PLANE)
    for src, dst, i, hs in w_copies():
        remote(src, dst, w_ss.at[i, hs], w_rs.at[i, hs], other_core).start()
    for e in range(4):
        arrived(idx_v.at[e], i_rs.at[e])
    load_idx = pltpu.make_async_copy(idx_v, idx_s, s_sem)
    load_idx.start()
    other_plane(0)
    load_idx.wait()
    for u in range(4):
        arrived(qbuf.at[u], q_rs.at[u])
    for count, unit, out1, out2 in own_kinds:

        def own_plane(n, carry, unit=unit, out1=out1, out2=out2):
            u, e = unit(n)
            query_blocks(0, PER_GROUP, 3, plane_part, u, e, 0, out1, out2)
            spread(1, 2 * u, 2 * u + 2)
            pass_on(0, 2 * u, 2 * u + 2)
            return carry

        lax.fori_loop(0, count, own_plane, 0)
    other_z(0)
    for count, unit, out1, out2 in own_kinds:

        def own_far(n, carry, unit=unit, out1=out1, out2=out2):
            u, e = unit(n)
            query_blocks(0, PER_GROUP, 6, z_part, u, e, 0, out1, out2)
            for args in o_copies(u, e, 0, range(3)):
                send_or_copy(*args)
            return carry

        lax.fori_loop(0, count, own_far, 0)
    pass_on(1, 0, 1)
    other_plane(1)
    for u in range(4, 6):
        arrived(qbuf.at[u], q_rs.at[u])
    for count, unit, out1, out2 in shared_kinds:

        def shared_plane(n, carry, unit=unit, out1=out1, out2=out2):
            u, e = unit(n)
            query_blocks(0, PER_GROUP, 3, plane_part, u, e, 1, out1, out2)
            pass_on(1, u - 3, u - 2)
            return carry

        lax.fori_loop(0, count, shared_plane, 0)

    for src, dst, i, hs in w_copies():
        pltpu.make_async_copy(src, dst, w_ls.at[i, hs]).wait()
    for i in range(2):
        for hs, size in enumerate((256, 128)):
            arrived(wbuf[hs].at[pl.ds(pl.multiple_of((2 * (1 - c) + i) * size, size), size), :], w_rs.at[i, hs])
    att_arrived(0, range(3))

    def cols_at(n):
        return pl.ds(pl.multiple_of(n * CHUNK, CHUNK), CHUNK)

    def project_own(n, carry):
        sums[:, cols_at(n)] = jnp.dot(att_a[...], w_a[:, cols_at(n)], preferred_element_type=jnp.float32)
        return carry

    def project_and_pass(n, carry):
        project_own(n, carry)
        pass_on(1, n + 3, n + 4)
        return carry

    lax.fori_loop(0, 5, project_and_pass, 0)
    lax.fori_loop(5, CHUNKS, project_own, 0)
    other_z(1)
    for ks, first in (((1, 2), 3 * (1 - yl)), ((0,), 3 * yl)):
        for count, unit, out1, out2 in shared_kinds:

            def shared_far(n, carry, unit=unit, out1=out1, out2=out2):
                u, e = unit(n)
                query_blocks(first, 3, 3, z_part, u, e, 1, out1, out2)
                for args in o_copies(u, e, 1, ks):
                    send_or_copy(*args)
                return carry

            lax.fori_loop(0, count, shared_far, 0)

    def r_copy(n, k):
        rows = pl.ds(96 * k, 96)
        return remote(sbuf.at[rows, cols_at(n)], rbuf.at[rows, cols_at(n)], r_ss.at[n, k], r_rs.at[n, k], partner[k])

    def project_theirs(n, carry):
        r = jnp.dot(att_c[:192], w_c[:, cols_at(n)], preferred_element_type=jnp.float32)
        sbuf[:, cols_at(n)] = (r + sums[:192, cols_at(n)]).astype(jnp.bfloat16)
        for k in range(2):
            r_copy(n, k).start()
        return carry

    def project_mine(n, carry):
        r = jnp.dot(att_c[192:], w_c[:, cols_at(n)], preferred_element_type=jnp.float32)
        sums[192:, cols_at(n)] = r + sums[192:, cols_at(n)]
        return carry

    def finish(n, carry):
        for k in range(2):
            r_copy(n, k).wait()
        total = sums[192:, cols_at(n)] + rbuf[:, cols_at(n)].astype(jnp.float32)
        out_ref[:, cols_at(n)] = total.astype(jnp.bfloat16)
        return carry

    att_arrived(1, (1, 2))
    lax.fori_loop(0, CHUNKS, project_theirs, 0)
    att_arrived(1, (0,))
    lax.fori_loop(0, CHUNKS, project_mine, 0)
    lax.fori_loop(0, CHUNKS, finish, 0)

    for copies in dealt:
        for args in copies():
            sent(*args)
    for src, dst, i, hs in w_copies():
        remote(src, dst, w_ss.at[i, hs], w_rs.at[i, hs], other_core).wait_send()

    def done(g, carry):
        for hs in range(2):
            plane_forward(hs, g).wait_send()

            @pl.when(has_high & to_high(hs, g))
            def _():
                z_copy(0, hs, g).wait_send()

            @pl.when(has_low & to_low(hs, g))
            def _():
                z_copy(1, hs, g).wait_send()

            for way in range(2):

                @pl.when(gets(way, hs, g))
                def _():
                    z_forward(way, hs, g).wait_send()

        return carry

    lax.fori_loop(0, PLANE, done, 0)

    def o_done(u, e, hs):
        for args in o_copies(u, e, hs, range(3)):
            sent(*args)

    def own_done(n, carry):
        o_done(n, n, 0)
        return carry

    def shared_done(n, carry):
        o_done(4 + n, 2 * yh + n, 1)
        return carry

    lax.fori_loop(0, 4, own_done, 0)
    lax.fori_loop(0, 2, shared_done, 0)


def per_device(queries, keys, values, block_mask, out_weight):
    dma = pltpu.SemaphoreType.DMA
    bf16, f32 = jnp.bfloat16, jnp.float32
    rows, piece = (GROUP, HEAD_DIM), (PER_GROUP, BLK, HEAD_DIM)
    scratch = [
        pltpu.VMEM((2, PLANE, *piece), bf16), pltpu.VMEM((2, PLANE, *piece), bf16),
        pltpu.VMEM((2, 2, PLANE, *piece), bf16), pltpu.VMEM((2, 2, PLANE, *piece), bf16),
        pltpu.VMEM((6, *piece), bf16),
        pltpu.VMEM((8, 256), jnp.int32),
        pltpu.VMEM((4, 8, 256), jnp.int32),
        pltpu.SMEM((4, 8, 256), jnp.int32),
        pltpu.VMEM((1024, WIDTH), bf16), pltpu.VMEM((512, WIDTH), bf16),
        pltpu.VMEM((6, *rows), f32),
        pltpu.VMEM((6, *rows), f32),
        pltpu.VMEM((6, *rows), f32),
        pltpu.VMEM((6, *rows), bf16),
        pltpu.VMEM((384, 1024), bf16), pltpu.VMEM((384, 512), bf16),
        pltpu.VMEM((384, WIDTH), f32),
        pltpu.VMEM((192, WIDTH), bf16),
        pltpu.VMEM((192, WIDTH), bf16),
        dma((2, 2, 4)), dma((2, 3)), dma((2, 2)), dma((2, 8)), dma((2, 2, 8)), dma((2, 2, 8)), dma((2, 2)),
        dma((6, 2, 3)), dma((CHUNKS, 2)),
        dma((2, 8)), dma((2, 8)), dma((6,)), dma((4,)), dma((2, 2, 8)), dma((2, 2, 8)), dma((2, 2)), dma((2, 2)),
        dma((2, 3)), dma((CHUNKS, 2)), dma,
    ]
    any_space = pl.BlockSpec(memory_space=pl.ANY)
    vmem = pl.BlockSpec(memory_space=pltpu.VMEM)
    by_block = [a.reshape(PER_GROUP, BLK, GROUP) for a in (queries, keys, values)]
    return pl.pallas_call(
        kernel,
        out_shape=jax.ShapeDtypeStruct((192, WIDTH), bf16),
        in_specs=[any_space, any_space, any_space, vmem, any_space],
        out_specs=vmem,
        scratch_shapes=scratch,
        compiler_params=pltpu.CompilerParams(
            collective_id=0, has_side_effects=True, vmem_limit_bytes=60 * 2**20
        ),
        name="attention",
    )(*by_block, block_mask, out_weight)


def solution(mesh):
    in_specs = (
        P("frame", "head"),
        P("frame", "head"),
        P("frame", "head"),
        P("frame", None),
        P("head", None),
    )
    out_specs = P(("frame", "head"), None)
    return jax.shard_map(
        per_device, mesh=mesh, in_specs=in_specs, out_specs=out_specs, check_vma=False
    )
```

```python
import math

import jax
import jax.numpy as jnp
from jax import lax
from jax.experimental import pallas as pl
from jax.experimental.pallas import tpu as pltpu
from jax.sharding import PartitionSpec as P

HEAD_DIM = 128
BLK = 128
GROUP = 768
PER_GROUP = GROUP // BLK
WIDTH = 3072
HEADS_CHIP = 12
PLANE = 8
CHUNK = 512
CHUNKS = WIDTH // CHUNK
EXP2_SCALE = HEAD_DIM ** (-0.5) * math.log2(math.e)
NEG = -1e30
MESH = pl.DeviceIdType.MESH


def live_blocks(mask):
    lane = lax.broadcasted_iota(jnp.int32, mask.shape, 1)
    at = lax.rem(lane, PER_GROUP)
    lanes = mask.shape[1]

    def ahead(value, by):
        return pltpu.roll(value, (lanes - by) % lanes, 1)

    before = jnp.where(at == 0, ahead(mask, PER_GROUP - 1), ahead(mask, lanes - 1))
    first = jnp.where((mask > 0) & (before == 0), at, 0)
    total = first
    for n in range(1, PER_GROUP):
        total = total + ahead(first, n)
    total = jnp.where((at == 0) & (lane < lanes - PER_GROUP), total, 0)
    shared = total
    for n in range(1, PER_GROUP):
        shared = shared + ahead(total, lanes - n)
    return lax.rem(shared + at, PER_GROUP)


def kernel(
    q_hbm, k_hbm, v_hbm, mask_ref, w_hbm, out_ref,
    plane_a, plane_c, z_a, z_c, qbuf, blocks_ref, idx_v, idx_s, w_a, w_c, acc, top_s, sum_s, obuf, att_a, att_c,
    sums, sbuf, rbuf,
    kv_ss, q_ss, i_ss, pf_ss, z_ss, zf_ss, w_ss, wx_ss, wg_ss, wf_ss, o_ss, oc_ss, r_ss,
    p_rs, pf_rs, q_rs, i_rs, z_rs, zf_rs, w_rs, w_ls, wx_rs, wg_rs, wf_rs, a_rs, ac_rs, r_rs, s_sem,
):
    plane, zbuf, wbuf = (plane_a, plane_c), (z_a, z_c), (w_a, w_c)
    f = lax.axis_index("frame")
    h = lax.axis_index("head")
    z, yh, x = f // 8, lax.rem(f // 4, 2), lax.rem(f, 4)
    yl, c = h // 2, lax.rem(h, 2)
    g_me = lax.rem(f, 8)
    has_low, has_high = z > 0, z < 3

    def device(z_, g_, yl_, c_):
        return {"frame": z_ * 8 + g_, "head": yl_ * 2 + c_}

    other_core = device(z, g_me, yl, 1 - c)

    def remote(src, dst, ss, rs, target):
        return pltpu.make_async_remote_copy(
            src_ref=src, dst_ref=dst, send_sem=ss, recv_sem=rs, device_id=target, device_id_type=MESH
        )

    def is_me(target):
        return (target["frame"] == f) & (target["head"] == h)

    def send_or_copy(src, dst, ss, rs, target):
        mine = is_me(target)

        @pl.when(jnp.logical_not(mine))
        def _():
            remote(src, dst, ss, rs, target).start()

        @pl.when(mine)
        def _():
            pltpu.make_async_copy(src, dst, rs).start()

    def sent(src, dst, ss, rs, target):
        @pl.when(jnp.logical_not(is_me(target)))
        def _():
            remote(src, dst, ss, rs, target).wait_send()

    def arrived(ref, sem):
        pltpu.make_async_copy(ref, ref, sem).wait()

    barrier = pltpu.get_barrier_semaphore()

    def greet(target):
        pl.semaphore_signal(barrier, inc=1, device_id=target, device_id_type=MESH)

    def greet_plane(i, carry):
        target = device(z, i // 4, lax.rem(i // 2, 2), lax.rem(i, 2))

        @pl.when(jnp.logical_not(is_me(target)))
        def _():
            greet(target)

        return carry

    lax.fori_loop(0, 4 * PLANE, greet_plane, 0)
    partner = [device(z, g_me, 1 - yl, c), device(z, (1 - yh) * 4 + x, 1 - yl, c)]
    low, high = device(z - 1, g_me, yl, c), device(z + 1, g_me, yl, c)
    for n in range(1, 4):
        greet(device(lax.rem(z + n, 4), g_me, yl, c))
    blocks_ref[...] = jnp.zeros_like(blocks_ref)
    blocks_ref[:PER_GROUP, : mask_ref.shape[1]] = mask_ref[...]
    blocks_ref[...] = live_blocks(blocks_ref[...])
    pl.semaphore_wait(barrier, 4 * PLANE - 1 + 3)

    e_me = x + yh * (3 - 2 * x)

    def kv_copies(hs):
        for n, (row, m) in enumerate(((0, 0), (0, 1), (1, 0), (1, 1))):
            to, i = lax.bitwise_xor(yh, row), lax.bitwise_xor(lax.rem(x, 2), m)
            at = pl.multiple_of((3 * i + (2 if hs else to)) * HEAD_DIM, HEAD_DIM)
            for t, src in enumerate((k_hbm, v_hbm)):
                yield (src.at[:, :, pl.ds(at, HEAD_DIM)], plane[hs].at[t, g_me],
                       kv_ss.at[t, hs, n], p_rs.at[hs, g_me], device(z, to * 4 + 2 * c + i, yl, t))

    def q_copies(hs):
        for i in range(2):
            for j in ((0, 1), (2,))[hs]:
                to, slot, core = (j, e_me, yh) if j < 2 else (yh, 4 + lax.rem(e_me, 2), e_me // 2)
                target = device(z, to * 4 + 2 * c + i, yl, core)
                yield blocks_ref, idx_v.at[slot], i_ss.at[i, j], i_rs.at[slot], target
                yield (q_hbm.at[:, :, pl.ds((3 * i + j) * HEAD_DIM, HEAD_DIM)], qbuf.at[slot],
                       q_ss.at[i, j], q_rs.at[slot], target)

    dealt = (lambda: kv_copies(0), lambda: q_copies(0), lambda: kv_copies(1), lambda: q_copies(1))
    for copies in dealt:
        for args in copies():
            send_or_copy(*args)

    def w_row(core, i, hs):
        return pl.multiple_of(yl * 512 + (2 * core + i) * 128 if hs else (2 * core + i) * 256, 128)

    def w_copies():
        for i in range(2):
            for hs, size in enumerate((256, 128)):
                yield (w_hbm.at[pl.ds(384 * i + 256 * hs, size), :],
                       wbuf[hs].at[pl.ds(w_row(c, i, hs), size), :], i, hs)

    for src, dst, i, hs in w_copies():
        pltpu.make_async_copy(src, dst, w_ls.at[i, hs]).start()

    def far_rows(core, part, size):
        return pl.ds(pl.multiple_of((1 - yl) * 512 + core * 256 + 64 * part, 64), size)

    quarter = jnp.where(c == 0, x, z)

    def w_across(k):
        row = pl.multiple_of((quarter // 2) * 384 + 256 + 64 * lax.rem(quarter, 2) + 32 * k, 32)
        there = pl.ds(pl.multiple_of(yl * 512 + c * 256 + 64 * quarter + 32 * k, 32), 32)
        return remote(w_hbm.at[pl.ds(row, 32), :], w_c.at[there, :], wx_ss.at[k], wx_rs.at[k], partner[k])

    def w_round(n):
        here = w_c.at[far_rows(c, quarter, 64), :]
        x_to = jnp.where(c == 0, lax.rem(x + n + 1, 4), x)
        z_to = jnp.where(c == 0, z, lax.rem(z + n + 1, 4))
        return remote(here, here, wg_ss.at[n], wg_rs.at[n], device(z_to, yh * 4 + x_to, yl, c))

    def w_swap():
        here = w_c.at[far_rows(c, 0, 256), :]
        return remote(here, here, wf_ss, wf_rs, other_core)

    for k in range(2):
        w_across(k).start()

    def frame_of(step):
        return lax.bitwise_xor(step, g_me)

    def to_high(hs, g):
        return ((yh == 0) | (g // 4 == 1)) if hs else (g >= 0)

    def to_low(hs, g):
        return ((yh == 1) | (g // 4 == 0)) if hs else (g >= 0)

    def z_copy(way, hs, g):
        return remote(plane[hs].at[c, g], zbuf[hs].at[way, c, g], z_ss.at[way, hs, g], z_rs.at[way, hs, g],
                      (high, low)[way])

    def plane_forward(hs, g):
        return remote(plane[hs].at[c, g], plane[hs].at[c, g], pf_ss.at[hs, g], pf_rs.at[hs, g], other_core)

    def z_forward(way, hs, g):
        return remote(zbuf[hs].at[way, c, g], zbuf[hs].at[way, c, g], zf_ss.at[way, hs, g], zf_rs.at[way, hs, g],
                      other_core)

    def spread(hs, first, last):
        def one(step, carry):
            g = frame_of(step)
            arrived(plane[hs].at[c, g], p_rs.at[hs, g])

            @pl.when(has_high & to_high(hs, g))
            def _():
                z_copy(0, hs, g).start()

            @pl.when(has_low & to_low(hs, g))
            def _():
                z_copy(1, hs, g).start()

            plane_forward(hs, g).start()
            return carry

        lax.fori_loop(first, last, one, 0)

    def gets(way, hs, g):
        return (has_low & to_high(hs, g), has_high & to_low(hs, g))[way]

    def pass_on(hs, first, last):
        def one(step, carry):
            g = frame_of(step)
            for way in range(2):

                @pl.when(gets(way, hs, g))
                def _():
                    arrived(zbuf[hs].at[way, c, g], z_rs.at[way, hs, g])
                    z_forward(way, hs, g).start()

            return carry

        lax.fori_loop(first, last, one, 0)

    def other_plane(hs):
        def one(g, carry):
            arrived(plane[hs].at[1 - c, g], pf_rs.at[hs, g])
            return carry

        lax.fori_loop(0, PLANE, one, 0)

    def other_z(hs):
        def one(g, carry):
            for way in range(2):

                @pl.when(gets(way, hs, g))
                def _():
                    arrived(zbuf[hs].at[way, 1 - c, g], zf_rs.at[way, hs, g])

            return carry

        lax.fori_loop(0, PLANE, one, 0)

    side_of = (c, yh)

    def frame_at(e, side):
        return e + side * (7 - 2 * e)

    def scores_of(q, keys):
        return lax.dot_general(q, keys, (((1,), (1,)), ((), ())), preferred_element_type=jnp.float32)

    def rows_at(qb):
        return pl.ds(pl.multiple_of(qb * BLK, BLK), BLK)

    def block(u, qb, g, way, distance, j=0):
        group = jnp.clip(z * PLANE + g + (2 * way - 1) * distance, 0, 4 * PLANE - 1)
        return idx_s[u, qb, group * PER_GROUP + j]

    def plane_part(u, e, hs, out1, out2, qb):
        side = side_of[hs]
        g = frame_at(e, side)

        def near_block(by, j=0):
            way = 1 - side if by > 0 else side
            return frame_at(e + by, side), block(u, qb, g, way, abs(by), j)

        near = [near_block(1, j) for j in range(3)] + [near_block(2), near_block(4)]
        if out1:
            near += [near_block(-1, j) for j in range(3)]
        if out2:
            near += [near_block(-2)]
        q = qbuf[u, qb]

        def taken(t):
            return jnp.concatenate(
                [plane[hs][t, g].reshape(GROUP, HEAD_DIM)] + [plane[hs][t, gg, b] for gg, b in near], axis=0
            )

        keys, vals = taken(0), taken(1)
        s = scores_of(q, keys)
        top = jnp.max(s, axis=1, keepdims=True)
        p = jnp.exp2((s - top) * EXP2_SCALE)
        total = jnp.sum(p, axis=1, keepdims=True)
        acc[u, rows_at(qb), :] = jnp.dot(p.astype(jnp.bfloat16), vals, preferred_element_type=jnp.float32)
        top_s[u, rows_at(qb), :] = jnp.broadcast_to(top, (BLK, HEAD_DIM))
        sum_s[u, rows_at(qb), :] = jnp.broadcast_to(total, (BLK, HEAD_DIM))

    def z_part(u, e, hs, out1, out2, qb):
        side = side_of[hs]
        g = frame_at(e, side)

        def far_block(distance, j=0):
            return side, frame_at(e + PLANE - distance, side), block(u, qb, g, side, distance, j)

        far = [(way, g, block(u, qb, g, way, 8)) for way in range(2)] + [far_block(4)]
        if not out2:
            far += [far_block(2)]
        if not out1:
            far += [far_block(1, j) for j in range(3)]
        q = qbuf[u, qb]
        keys, vals, valid = [], [], []
        for way, gg, b in far:
            ok = ((way == 0) & has_low) | ((way == 1) & has_high)
            w2 = jnp.where(ok, way, 1 - way)
            g2 = jnp.where(ok, gg, g)
            keys.append(zbuf[hs][w2, 0, g2, b])
            vals.append(zbuf[hs][w2, 1, g2, b])
            valid.append(jnp.where(ok, 0.0, NEG))
        s = scores_of(q, jnp.concatenate(keys, axis=0))
        s = jnp.concatenate(
            [s[:, n * BLK : (n + 1) * BLK] + valid[n] for n in range(len(far))], axis=1
        )
        old = top_s[u, rows_at(qb), :]
        top = jnp.maximum(old[:, :1], jnp.max(s, axis=1, keepdims=True))
        p = jnp.exp2((s - top) * EXP2_SCALE)
        keep = jnp.exp2((old - top) * EXP2_SCALE)
        total = sum_s[u, rows_at(qb), :] * keep + jnp.sum(p, axis=1, keepdims=True)
        o = acc[u, rows_at(qb), :] * keep + jnp.dot(
            p.astype(jnp.bfloat16), jnp.concatenate(vals, axis=0), preferred_element_type=jnp.float32
        )
        obuf[u, rows_at(qb), :] = (o / total).astype(jnp.bfloat16)

    def query_blocks(first, last, unroll, part, *unit):
        def one(qb, carry):
            part(*unit, first + qb)
            return carry

        lax.fori_loop(0, last, one, 0, unroll=unroll)

    def own_o_copies(u):
        cols = pl.ds(pl.multiple_of((2 * x + yh) * HEAD_DIM, HEAD_DIM), HEAD_DIM)
        x_to = u + c * (3 - 2 * u)
        here, across = c * 4 + x_to, (1 - c) * 4 + x_to
        for t in range(2):
            mine, theirs = (2 * yl + t) * 192, (2 * (1 - yl) + t) * 192
            parts = ((mine, 192, 192, here), (theirs, 96, 0, here), (theirs + 96, 96, 96, across))
            for k, (row, size, at, to) in enumerate(parts):
                yield (obuf.at[u, pl.ds(pl.multiple_of(row, 96), size), :], att_a.at[pl.ds(at, size), cols],
                       o_ss.at[u, t, k], a_rs.at[k], device(z, to, yl, t))

    def shared_o_copies(u, e):
        cols = pl.ds(pl.multiple_of(yl * 512 + x * HEAD_DIM, HEAD_DIM), HEAD_DIM)
        to = yh * 4 + e + yh * (3 - 2 * e)
        for yl_to in range(2):
            for t in range(2):
                yield (obuf.at[u, pl.ds((2 * yl_to + t) * 192, 192), :], att_c.at[:, cols],
                       oc_ss.at[u - 4, 2 * yl_to + t], ac_rs, device(z, to, yl_to, t))

    own_kinds = (
        (1, lambda n: (0, 0), False, False),
        (1, lambda n: (1, 1), True, False),
        (2, lambda n: (2 + n, 2 + n), True, True),
    )
    shared_kinds = (
        (1 - c, lambda n: (4, 0), False, False),
        (1 - c, lambda n: (5, 1), True, False),
        (2 * c, lambda n: (4 + n, 2 + n), True, True),
    )

    def units_ready(first, last):
        for u in range(first, last):
            arrived(idx_v.at[u], i_rs.at[u])
        load = pltpu.make_async_copy(idx_v.at[pl.ds(first, last - first)], idx_s.at[pl.ds(first, last - first)], s_sem)
        load.start()
        load.wait()
        for u in range(first, last):
            arrived(qbuf.at[u], q_rs.at[u])

    spread(0, 0, PLANE)
    for src, dst, i, hs in w_copies():
        remote(src, dst, w_ss.at[i, hs], w_rs.at[i, hs], other_core).start()
    other_plane(0)
    units_ready(0, 4)
    for count, unit, out1, out2 in own_kinds:

        def own_plane(n, carry, unit=unit, out1=out1, out2=out2):
            u, e = unit(n)
            query_blocks(0, PER_GROUP, 3, plane_part, u, e, 0, out1, out2)
            spread(1, 2 * u, 2 * u + 2)
            pass_on(0, 2 * u, 2 * u + 2)
            return carry

        lax.fori_loop(0, count, own_plane, 0)
    for k in range(2):
        w_across(k).wait_recv()
    for n in range(3):
        w_round(n).start()
    other_z(0)
    for count, unit, out1, out2 in own_kinds:

        def own_far(n, carry, unit=unit, out1=out1, out2=out2):
            u, e = unit(n)
            query_blocks(0, PER_GROUP, 6, z_part, u, e, 0, out1, out2)
            for args in own_o_copies(u):
                send_or_copy(*args)
            return carry

        lax.fori_loop(0, count, own_far, 0)
    pass_on(1, 0, 1)
    other_plane(1)
    units_ready(4, 6)
    for count, unit, out1, out2 in shared_kinds:

        def shared_plane(n, carry, unit=unit, out1=out1, out2=out2):
            u, e = unit(n)
            query_blocks(0, PER_GROUP, 3, plane_part, u, e, 1, out1, out2)
            pass_on(1, u - 3, u - 2)
            return carry

        lax.fori_loop(0, count, shared_plane, 0)

    for src, dst, i, hs in w_copies():
        pltpu.make_async_copy(src, dst, w_ls.at[i, hs]).wait()
    for i in range(2):
        for hs, size in enumerate((256, 128)):
            arrived(wbuf[hs].at[pl.ds(w_row(1 - c, i, hs), size), :], w_rs.at[i, hs])
    for k, (row, size) in enumerate(((192, 192), (0, 96), (96, 96))):
        arrived(att_a.at[pl.ds(row, size)], a_rs.at[k])

    def cols_at(n):
        return pl.ds(pl.multiple_of(n * CHUNK, CHUNK), CHUNK)

    def r_copy(n, k):
        rows = pl.ds(96 * k, 96)
        return remote(sbuf.at[rows, cols_at(n)], rbuf.at[rows, cols_at(n)], r_ss.at[n, k], r_rs.at[n, k], partner[k])

    def project_own(n, carry):
        r = jnp.dot(att_a[...], w_a[:, cols_at(n)], preferred_element_type=jnp.float32)
        sbuf[:, cols_at(n)] = r[:192].astype(jnp.bfloat16)
        sums[:, cols_at(n)] = r[192:]
        for k in range(2):
            r_copy(n, k).start()
        return carry

    def project_and_pass(n, carry):
        project_own(n, carry)
        pass_on(1, n + 3, n + 4)
        return carry

    lax.fori_loop(0, 5, project_and_pass, 0)
    lax.fori_loop(5, CHUNKS, project_own, 0)
    for n in range(3):
        arrived(w_c.at[far_rows(c, lax.rem(quarter + 3 - n, 4), 64), :], wg_rs.at[n])
    w_swap().start()
    other_z(1)
    for count, unit, out1, out2 in shared_kinds:

        def shared_far(n, carry, unit=unit, out1=out1, out2=out2):
            u, e = unit(n)
            query_blocks(0, PER_GROUP, 6, z_part, u, e, 1, out1, out2)
            for args in shared_o_copies(u, e):
                send_or_copy(*args)
            return carry

        lax.fori_loop(0, count, shared_far, 0)

    def finish(n, carry):
        for k in range(2):
            r_copy(n, k).wait()
        total = sums[:, cols_at(n)] + rbuf[:, cols_at(n)].astype(jnp.float32)
        total = total + jnp.dot(att_c[...], w_c[:, cols_at(n)], preferred_element_type=jnp.float32)
        out_ref[:, cols_at(n)] = total.astype(jnp.bfloat16)
        return carry

    arrived(w_c.at[far_rows(1 - c, 0, 256), :], wf_rs)
    arrived(att_c, ac_rs)
    lax.fori_loop(0, CHUNKS, finish, 0)

    for copies in dealt:
        for args in copies():
            sent(*args)
    for src, dst, i, hs in w_copies():
        remote(src, dst, w_ss.at[i, hs], w_rs.at[i, hs], other_core).wait_send()

    def done(g, carry):
        for hs in range(2):
            plane_forward(hs, g).wait_send()

            @pl.when(has_high & to_high(hs, g))
            def _():
                z_copy(0, hs, g).wait_send()

            @pl.when(has_low & to_low(hs, g))
            def _():
                z_copy(1, hs, g).wait_send()

            for way in range(2):

                @pl.when(gets(way, hs, g))
                def _():
                    z_forward(way, hs, g).wait_send()

        return carry

    lax.fori_loop(0, PLANE, done, 0)

    for k in range(2):
        w_across(k).wait_send()
    for n in range(3):
        w_round(n).wait_send()
    w_swap().wait_send()

    def own_done(u, carry):
        for args in own_o_copies(u):
            sent(*args)
        return carry

    def shared_done(n, carry):
        for args in shared_o_copies(4 + n, 2 * c + n):
            sent(*args)
        return carry

    lax.fori_loop(0, 4, own_done, 0)
    lax.fori_loop(0, 2, shared_done, 0)


def per_device(queries, keys, values, block_mask, out_weight):
    dma = pltpu.SemaphoreType.DMA
    bf16, f32 = jnp.bfloat16, jnp.float32
    rows, piece = (GROUP, HEAD_DIM), (PER_GROUP, BLK, HEAD_DIM)
    scratch = [
        pltpu.VMEM((2, PLANE, *piece), bf16), pltpu.VMEM((2, PLANE, *piece), bf16),
        pltpu.VMEM((2, 2, PLANE, *piece), bf16), pltpu.VMEM((2, 2, PLANE, *piece), bf16),
        pltpu.VMEM((6, *piece), bf16),
        pltpu.VMEM((8, 256), jnp.int32),
        pltpu.VMEM((6, 8, 256), jnp.int32),
        pltpu.SMEM((6, 8, 256), jnp.int32),
        pltpu.VMEM((1024, WIDTH), bf16), pltpu.VMEM((1024, WIDTH), bf16),
        pltpu.VMEM((6, *rows), f32),
        pltpu.VMEM((6, *rows), f32),
        pltpu.VMEM((6, *rows), f32),
        pltpu.VMEM((6, *rows), bf16),
        pltpu.VMEM((384, 1024), bf16), pltpu.VMEM((192, 1024), bf16),
        pltpu.VMEM((192, WIDTH), f32),
        pltpu.VMEM((192, WIDTH), bf16),
        pltpu.VMEM((192, WIDTH), bf16),
        dma((2, 2, 4)), dma((2, 3)), dma((2, 3)), dma((2, 8)), dma((2, 2, 8)), dma((2, 2, 8)), dma((2, 2)),
        dma((2,)), dma((3,)), dma, dma((4, 2, 3)), dma((2, 4)), dma((CHUNKS, 2)),
        dma((2, 8)), dma((2, 8)), dma((6,)), dma((6,)), dma((2, 2, 8)), dma((2, 2, 8)), dma((2, 2)), dma((2, 2)),
        dma((2,)), dma((3,)), dma, dma((3,)), dma, dma((CHUNKS, 2)), dma,
    ]
    any_space = pl.BlockSpec(memory_space=pl.ANY)
    vmem = pl.BlockSpec(memory_space=pltpu.VMEM)
    by_block = [a.reshape(PER_GROUP, BLK, GROUP) for a in (queries, keys, values)]
    return pl.pallas_call(
        kernel,
        out_shape=jax.ShapeDtypeStruct((192, WIDTH), bf16),
        in_specs=[any_space, any_space, any_space, vmem, any_space],
        out_specs=vmem,
        scratch_shapes=scratch,
        compiler_params=pltpu.CompilerParams(
            collective_id=0, has_side_effects=True, vmem_limit_bytes=60 * 2**20
        ),
        name="attention",
    )(*by_block, block_mask, out_weight)


def solution(mesh):
    in_specs = (
        P("frame", "head"),
        P("frame", "head"),
        P("frame", "head"),
        P("frame", None),
        P("head", None),
    )
    out_specs = P(("frame", "head"), None)
    return jax.shard_map(
        per_device, mesh=mesh, in_specs=in_specs, out_specs=out_specs, check_vma=False
    )
```

```python
import math

import jax
import jax.numpy as jnp
from jax import lax
from jax.experimental import pallas as pl
from jax.experimental.pallas import tpu as pltpu
from jax.sharding import PartitionSpec as P

HEAD_DIM = 128
BLK = 128
GROUP = 768
PER_GROUP = GROUP // BLK
WIDTH = 3072
HEADS_CHIP = 12
PLANE = 8
CHUNK = 512
CHUNKS = WIDTH // CHUNK
EXP2_SCALE = HEAD_DIM ** (-0.5) * math.log2(math.e)
NEG = -1e30
MESH = pl.DeviceIdType.MESH


def live_blocks(mask):
    lane = lax.broadcasted_iota(jnp.int32, mask.shape, 1)
    at = lax.rem(lane, PER_GROUP)
    lanes = mask.shape[1]

    def ahead(value, by):
        return pltpu.roll(value, (lanes - by) % lanes, 1)

    before = jnp.where(at == 0, ahead(mask, PER_GROUP - 1), ahead(mask, lanes - 1))
    first = jnp.where((mask > 0) & (before == 0), at, 0)
    total = first
    for n in range(1, PER_GROUP):
        total = total + ahead(first, n)
    total = jnp.where((at == 0) & (lane < lanes - PER_GROUP), total, 0)
    shared = total
    for n in range(1, PER_GROUP):
        shared = shared + ahead(total, lanes - n)
    return lax.rem(shared + at, PER_GROUP)


def kernel(
    q_hbm, k_hbm, v_hbm, mask_ref, w_hbm, out_ref,
    plane_a, plane_c, z_a, z_c, qbuf, blocks_ref, idx_v, idx_s, w_a, w_c, acc, top_s, sum_s, obuf, att_a, att_c,
    sums, sbuf, rbuf,
    kv_ss, q_ss, i_ss, pf_ss, z_ss, zf_ss, w_ss, wx_ss, wg_ss, wf_ss, o_ss, oc_ss, r_ss,
    p_rs, pf_rs, q_rs, i_rs, z_rs, zf_rs, w_rs, w_ls, wx_rs, wg_rs, wf_rs, a_rs, ac_rs, r_rs, s_sem,
):
    plane, zbuf, wbuf = (plane_a, plane_c), (z_a, z_c), (w_a, w_c)
    f = lax.axis_index("frame")
    h = lax.axis_index("head")
    z, yh, x = f // 8, lax.rem(f // 4, 2), lax.rem(f, 4)
    yl, c = h // 2, lax.rem(h, 2)
    g_me = lax.rem(f, 8)
    has_low, has_high = z > 0, z < 3

    def device(z_, g_, yl_, c_):
        return {"frame": z_ * 8 + g_, "head": yl_ * 2 + c_}

    other_core = device(z, g_me, yl, 1 - c)

    def remote(src, dst, ss, rs, target):
        return pltpu.make_async_remote_copy(
            src_ref=src, dst_ref=dst, send_sem=ss, recv_sem=rs, device_id=target, device_id_type=MESH
        )

    def is_me(target):
        return (target["frame"] == f) & (target["head"] == h)

    def send_or_copy(src, dst, ss, rs, target):
        mine = is_me(target)

        @pl.when(jnp.logical_not(mine))
        def _():
            remote(src, dst, ss, rs, target).start()

        @pl.when(mine)
        def _():
            pltpu.make_async_copy(src, dst, rs).start()

    def sent(src, dst, ss, rs, target):
        @pl.when(jnp.logical_not(is_me(target)))
        def _():
            remote(src, dst, ss, rs, target).wait_send()

    def arrived(ref, sem):
        pltpu.make_async_copy(ref, ref, sem).wait()

    barrier = pltpu.get_barrier_semaphore()

    def greet(target):
        pl.semaphore_signal(barrier, inc=1, device_id=target, device_id_type=MESH)

    dealer = x // 2

    def greet_plane(g, carry):
        greet(device(z, g, yl, jnp.where(g == g_me, 1 - c, dealer)))
        return carry

    lax.fori_loop(0, PLANE, greet_plane, 0)
    partner = [device(z, g_me, 1 - yl, c), device(z, (1 - yh) * 4 + x, 1 - yl, c)]
    for target in partner:
        greet(target)
    low, high = device(z - 1, g_me, yl, c), device(z + 1, g_me, yl, c)
    for n in range(1, 4):
        greet(device(lax.rem(z + n, 4), g_me, yl, c))
    blocks_ref[...] = jnp.zeros_like(blocks_ref)
    blocks_ref[:PER_GROUP, : mask_ref.shape[1]] = mask_ref[...]
    blocks_ref[...] = live_blocks(blocks_ref[...])
    pl.semaphore_wait(barrier, jnp.where(dealer == c, 7, 9) + 2 + 3)

    e_me = x + yh * (3 - 2 * x)

    def kv_copies(hs):
        for n, (row, m) in enumerate(((0, 0), (0, 1), (1, 0), (1, 1))):
            to, i = lax.bitwise_xor(yh, row), lax.bitwise_xor(lax.rem(x, 2), m)
            at = pl.multiple_of((3 * i + (2 if hs else to)) * HEAD_DIM, HEAD_DIM)
            for t, src in enumerate((k_hbm, v_hbm)):
                yield (src.at[:, :, pl.ds(at, HEAD_DIM)], plane[hs].at[t, g_me],
                       kv_ss.at[t, hs, n], p_rs.at[hs, g_me], device(z, to * 4 + 2 * c + i, yl, t))

    def q_copies(hs):
        for i in range(2):
            for j in ((0, 1), (2,))[hs]:
                to, slot, core = (j, e_me, yh) if j < 2 else (yh, 4 + lax.rem(e_me, 2), e_me // 2)
                target = device(z, to * 4 + 2 * c + i, yl, core)
                yield blocks_ref, idx_v.at[slot], i_ss.at[i, j], i_rs.at[slot], target
                yield (q_hbm.at[:, :, pl.ds((3 * i + j) * HEAD_DIM, HEAD_DIM)], qbuf.at[slot],
                       q_ss.at[i, j], q_rs.at[slot], target)

    dealt = (lambda: kv_copies(0), lambda: q_copies(0), lambda: kv_copies(1), lambda: q_copies(1))
    for copies in dealt:
        for args in copies():
            send_or_copy(*args)

    def w_row(core, i, hs):
        return pl.multiple_of(yl * 512 + (2 * core + i) * 128 if hs else (2 * core + i) * 256, 128)

    def w_copies():
        for i in range(2):
            for hs, size in enumerate((256, 128)):
                yield (w_hbm.at[pl.ds(384 * i + 256 * hs, size), :],
                       wbuf[hs].at[pl.ds(w_row(c, i, hs), size), :], i, hs)

    for src, dst, i, hs in w_copies():
        pltpu.make_async_copy(src, dst, w_ls.at[i, hs]).start()

    def far_rows(core, part, size):
        return pl.ds(pl.multiple_of((1 - yl) * 512 + core * 256 + 64 * part, 64), size)

    quarter = jnp.where(c == 0, x, z)

    def w_across(k):
        row = pl.multiple_of((quarter // 2) * 384 + 256 + 64 * lax.rem(quarter, 2) + 32 * k, 32)
        there = pl.ds(pl.multiple_of(yl * 512 + c * 256 + 64 * quarter + 32 * k, 32), 32)
        return remote(w_hbm.at[pl.ds(row, 32), :], w_c.at[there, :], wx_ss.at[k], wx_rs.at[k], partner[k])

    def w_round(n):
        here = w_c.at[far_rows(c, quarter, 64), :]
        x_to = jnp.where(c == 0, lax.rem(x + n + 1, 4), x)
        z_to = jnp.where(c == 0, z, lax.rem(z + n + 1, 4))
        return remote(here, here, wg_ss.at[n], wg_rs.at[n], device(z_to, yh * 4 + x_to, yl, c))

    def w_swap():
        here = w_c.at[far_rows(c, 0, 256), :]
        return remote(here, here, wf_ss, wf_rs, other_core)

    for k in range(2):
        w_across(k).start()

    def frame_of(step):
        return lax.bitwise_xor(step, g_me)

    def to_high(hs, g):
        return ((yh == 0) | (g // 4 == 1)) if hs else (g >= 0)

    def to_low(hs, g):
        return ((yh == 1) | (g // 4 == 0)) if hs else (g >= 0)

    def z_copy(way, hs, g):
        return remote(plane[hs].at[c, g], zbuf[hs].at[way, c, g], z_ss.at[way, hs, g], z_rs.at[way, hs, g],
                      (high, low)[way])

    def plane_forward(hs, g):
        return remote(plane[hs].at[c, g], plane[hs].at[c, g], pf_ss.at[hs, g], pf_rs.at[hs, g], other_core)

    def z_forward(way, hs, g):
        return remote(zbuf[hs].at[way, c, g], zbuf[hs].at[way, c, g], zf_ss.at[way, hs, g], zf_rs.at[way, hs, g],
                      other_core)

    def spread(hs, first, last):
        def one(step, carry):
            g = frame_of(step)
            arrived(plane[hs].at[c, g], p_rs.at[hs, g])

            @pl.when(has_high & to_high(hs, g))
            def _():
                z_copy(0, hs, g).start()

            @pl.when(has_low & to_low(hs, g))
            def _():
                z_copy(1, hs, g).start()

            plane_forward(hs, g).start()
            return carry

        lax.fori_loop(first, last, one, 0)

    def gets(way, hs, g):
        return (has_low & to_high(hs, g), has_high & to_low(hs, g))[way]

    def pass_on(hs, first, last):
        def one(step, carry):
            g = frame_of(step)
            for way in range(2):

                @pl.when(gets(way, hs, g))
                def _():
                    arrived(zbuf[hs].at[way, c, g], z_rs.at[way, hs, g])
                    z_forward(way, hs, g).start()

            return carry

        lax.fori_loop(first, last, one, 0)

    def other_plane(hs):
        def one(g, carry):
            arrived(plane[hs].at[1 - c, g], pf_rs.at[hs, g])
            return carry

        lax.fori_loop(0, PLANE, one, 0)

    def other_z(hs):
        def one(g, carry):
            for way in range(2):

                @pl.when(gets(way, hs, g))
                def _():
                    arrived(zbuf[hs].at[way, 1 - c, g], zf_rs.at[way, hs, g])

            return carry

        lax.fori_loop(0, PLANE, one, 0)

    side_of = (c, yh)

    def frame_at(e, side):
        return e + side * (7 - 2 * e)

    def scores_of(q, keys):
        return lax.dot_general(q, keys, (((1,), (1,)), ((), ())), preferred_element_type=jnp.float32)

    def rows_at(qb):
        return pl.ds(pl.multiple_of(qb * BLK, BLK), BLK)

    def block(u, qb, g, way, distance, j=0):
        group = jnp.clip(z * PLANE + g + (2 * way - 1) * distance, 0, 4 * PLANE - 1)
        return idx_s[u, qb, group * PER_GROUP + j]

    def plane_part(u, e, hs, out1, out2, qb):
        side = side_of[hs]
        g = frame_at(e, side)

        def near_block(by, j=0):
            way = 1 - side if by > 0 else side
            return frame_at(e + by, side), block(u, qb, g, way, abs(by), j)

        near = [near_block(1, j) for j in range(3)] + [near_block(2), near_block(4)]
        if out1:
            near += [near_block(-1, j) for j in range(3)]
        if out2:
            near += [near_block(-2)]
        q = qbuf[u, qb]

        def taken(t):
            return jnp.concatenate(
                [plane[hs][t, g].reshape(GROUP, HEAD_DIM)] + [plane[hs][t, gg, b] for gg, b in near], axis=0
            )

        keys, vals = taken(0), taken(1)
        s = scores_of(q, keys)
        top = jnp.max(s, axis=1, keepdims=True)
        p = jnp.exp2((s - top) * EXP2_SCALE)
        total = jnp.sum(p, axis=1, keepdims=True)
        acc[u, rows_at(qb), :] = jnp.dot(p.astype(jnp.bfloat16), vals, preferred_element_type=jnp.float32)
        top_s[u, rows_at(qb), :] = jnp.broadcast_to(top, (BLK, HEAD_DIM))
        sum_s[u, rows_at(qb), :] = jnp.broadcast_to(total, (BLK, HEAD_DIM))

    def z_part(u, e, hs, out1, out2, qb):
        side = side_of[hs]
        g = frame_at(e, side)

        def far_block(distance, j=0):
            return side, frame_at(e + PLANE - distance, side), block(u, qb, g, side, distance, j)

        far = [(way, g, block(u, qb, g, way, 8)) for way in range(2)] + [far_block(4)]
        if not out2:
            far += [far_block(2)]
        if not out1:
            far += [far_block(1, j) for j in range(3)]
        q = qbuf[u, qb]
        keys, vals, valid = [], [], []
        for way, gg, b in far:
            ok = ((way == 0) & has_low) | ((way == 1) & has_high)
            w2 = jnp.where(ok, way, 1 - way)
            g2 = jnp.where(ok, gg, g)
            keys.append(zbuf[hs][w2, 0, g2, b])
            vals.append(zbuf[hs][w2, 1, g2, b])
            valid.append(jnp.where(ok, 0.0, NEG))
        s = scores_of(q, jnp.concatenate(keys, axis=0))
        s = jnp.concatenate(
            [s[:, n * BLK : (n + 1) * BLK] + valid[n] for n in range(len(far))], axis=1
        )
        old = top_s[u, rows_at(qb), :]
        top = jnp.maximum(old[:, :1], jnp.max(s, axis=1, keepdims=True))
        p = jnp.exp2((s - top) * EXP2_SCALE)
        keep = jnp.exp2((old - top) * EXP2_SCALE)
        total = sum_s[u, rows_at(qb), :] * keep + jnp.sum(p, axis=1, keepdims=True)
        o = acc[u, rows_at(qb), :] * keep + jnp.dot(
            p.astype(jnp.bfloat16), jnp.concatenate(vals, axis=0), preferred_element_type=jnp.float32
        )
        obuf[u, rows_at(qb), :] = (o / total).astype(jnp.bfloat16)

    def query_blocks(first, last, unroll, part, *unit):
        def one(qb, carry):
            part(*unit, first + qb)
            return carry

        lax.fori_loop(0, last, one, 0, unroll=unroll)

    def own_o_copies(u):
        cols = pl.ds(pl.multiple_of((2 * x + yh) * HEAD_DIM, HEAD_DIM), HEAD_DIM)
        x_to = u + c * (3 - 2 * u)
        here, across = c * 4 + x_to, (1 - c) * 4 + x_to
        for t in range(2):
            mine, theirs = (2 * yl + t) * 192, (2 * (1 - yl) + t) * 192
            parts = ((mine, 192, 192, here), (theirs, 96, 0, here), (theirs + 96, 96, 96, across))
            for k, (row, size, at, to) in enumerate(parts):
                yield (obuf.at[u, pl.ds(pl.multiple_of(row, 96), size), :], att_a.at[pl.ds(at, size), cols],
                       o_ss.at[u, t, k], a_rs.at[k], device(z, to, yl, t))

    def shared_o_copies(u, e):
        cols = pl.ds(pl.multiple_of(yl * 512 + x * HEAD_DIM, HEAD_DIM), HEAD_DIM)
        to = yh * 4 + e + yh * (3 - 2 * e)
        for yl_to in range(2):
            for t in range(2):
                yield (obuf.at[u, pl.ds((2 * yl_to + t) * 192, 192), :], att_c.at[:, cols],
                       oc_ss.at[u - 4, 2 * yl_to + t], ac_rs, device(z, to, yl_to, t))

    own_kinds = (
        (1, lambda n: (0, 0), False, False),
        (1, lambda n: (1, 1), True, False),
        (2, lambda n: (2 + n, 2 + n), True, True),
    )
    shared_kinds = (
        (1 - c, lambda n: (4, 0), False, False),
        (1 - c, lambda n: (5, 1), True, False),
        (2 * c, lambda n: (4 + n, 2 + n), True, True),
    )

    def units_ready(first, last):
        for u in range(first, last):
            arrived(idx_v.at[u], i_rs.at[u])
        load = pltpu.make_async_copy(idx_v.at[pl.ds(first, last - first)], idx_s.at[pl.ds(first, last - first)], s_sem)
        load.start()
        load.wait()
        for u in range(first, last):
            arrived(qbuf.at[u], q_rs.at[u])

    spread(0, 0, PLANE)
    for src, dst, i, hs in w_copies():
        remote(src, dst, w_ss.at[i, hs], w_rs.at[i, hs], other_core).start()
    other_plane(0)
    units_ready(0, 4)
    for count, unit, out1, out2 in own_kinds:

        def own_plane(n, carry, unit=unit, out1=out1, out2=out2):
            u, e = unit(n)
            query_blocks(0, PER_GROUP, 3, plane_part, u, e, 0, out1, out2)
            spread(1, u, u + 1)
            pass_on(0, 2 * u, 2 * u + 2)
            return carry

        lax.fori_loop(0, count, own_plane, 0)
    other_z(0)
    for count, unit, out1, out2 in own_kinds:

        def own_far(n, carry, unit=unit, out1=out1, out2=out2):
            u, e = unit(n)
            query_blocks(0, PER_GROUP, 6, z_part, u, e, 0, out1, out2)
            for args in own_o_copies(u):
                send_or_copy(*args)
            return carry

        lax.fori_loop(0, count, own_far, 0)
    spread(1, 4, PLANE)
    pass_on(1, 0, 1)
    other_plane(1)
    units_ready(4, 6)
    for count, unit, out1, out2 in shared_kinds:

        def shared_plane(n, carry, unit=unit, out1=out1, out2=out2):
            u, e = unit(n)
            query_blocks(0, PER_GROUP, 3, plane_part, u, e, 1, out1, out2)
            pass_on(1, u - 3, u - 2)
            return carry

        lax.fori_loop(0, count, shared_plane, 0)

    for src, dst, i, hs in w_copies():
        pltpu.make_async_copy(src, dst, w_ls.at[i, hs]).wait()
    for i in range(2):
        for hs, size in enumerate((256, 128)):
            arrived(wbuf[hs].at[pl.ds(w_row(1 - c, i, hs), size), :], w_rs.at[i, hs])
    for k, (row, size) in enumerate(((192, 192), (0, 96), (96, 96))):
        arrived(att_a.at[pl.ds(row, size)], a_rs.at[k])

    def cols_at(n):
        return pl.ds(pl.multiple_of(n * CHUNK, CHUNK), CHUNK)

    def r_copy(n, k):
        rows = pl.ds(96 * k, 96)
        return remote(sbuf.at[rows, cols_at(n)], rbuf.at[rows, cols_at(n)], r_ss.at[n, k], r_rs.at[n, k], partner[k])

    def project_own(n, carry):
        r = jnp.dot(att_a[...], w_a[:, cols_at(n)], preferred_element_type=jnp.float32)
        sbuf[:, cols_at(n)] = r[:192].astype(jnp.bfloat16)
        sums[:, cols_at(n)] = r[192:]
        for k in range(2):
            r_copy(n, k).start()
        return carry

    def project_and_pass(n, carry):
        project_own(n, carry)
        pass_on(1, n + 3, n + 4)
        return carry

    for k in range(2):
        w_across(k).wait_recv()
    for n in range(3):
        w_round(n).start()
    lax.fori_loop(0, 5, project_and_pass, 0)
    lax.fori_loop(5, CHUNKS, project_own, 0)
    for n in range(3):
        arrived(w_c.at[far_rows(c, lax.rem(quarter + 3 - n, 4), 64), :], wg_rs.at[n])
    w_swap().start()
    other_z(1)
    for count, unit, out1, out2 in shared_kinds:

        def shared_far(n, carry, unit=unit, out1=out1, out2=out2):
            u, e = unit(n)
            query_blocks(0, PER_GROUP, 6, z_part, u, e, 1, out1, out2)
            for args in shared_o_copies(u, e):
                send_or_copy(*args)
            return carry

        lax.fori_loop(0, count, shared_far, 0)

    def finish(n, carry):
        for k in range(2):
            r_copy(n, k).wait()
        total = sums[:, cols_at(n)] + rbuf[:, cols_at(n)].astype(jnp.float32)
        total = total + jnp.dot(att_c[...], w_c[:, cols_at(n)], preferred_element_type=jnp.float32)
        out_ref[:, cols_at(n)] = total.astype(jnp.bfloat16)
        return carry

    for copies in dealt:
        for args in copies():
            sent(*args)
    for src, dst, i, hs in w_copies():
        remote(src, dst, w_ss.at[i, hs], w_rs.at[i, hs], other_core).wait_send()

    def done(g, carry):
        for hs in range(2):
            plane_forward(hs, g).wait_send()

            @pl.when(has_high & to_high(hs, g))
            def _():
                z_copy(0, hs, g).wait_send()

            @pl.when(has_low & to_low(hs, g))
            def _():
                z_copy(1, hs, g).wait_send()

            for way in range(2):

                @pl.when(gets(way, hs, g))
                def _():
                    z_forward(way, hs, g).wait_send()

        return carry

    lax.fori_loop(0, PLANE, done, 0)

    for k in range(2):
        w_across(k).wait_send()
    for n in range(3):
        w_round(n).wait_send()
    w_swap().wait_send()

    def own_done(u, carry):
        for args in own_o_copies(u):
            sent(*args)
        return carry

    lax.fori_loop(0, 4, own_done, 0)
    arrived(w_c.at[far_rows(1 - c, 0, 256), :], wf_rs)
    arrived(att_c, ac_rs)
    lax.fori_loop(0, CHUNKS, finish, 0)

    def shared_done(n, carry):
        for args in shared_o_copies(4 + n, 2 * c + n):
            sent(*args)
        return carry

    lax.fori_loop(0, 2, shared_done, 0)


def per_device(queries, keys, values, block_mask, out_weight):
    dma = pltpu.SemaphoreType.DMA
    bf16, f32 = jnp.bfloat16, jnp.float32
    rows, piece = (GROUP, HEAD_DIM), (PER_GROUP, BLK, HEAD_DIM)
    scratch = [
        pltpu.VMEM((2, PLANE, *piece), bf16), pltpu.VMEM((2, PLANE, *piece), bf16),
        pltpu.VMEM((2, 2, PLANE, *piece), bf16), pltpu.VMEM((2, 2, PLANE, *piece), bf16),
        pltpu.VMEM((6, *piece), bf16),
        pltpu.VMEM((8, 256), jnp.int32),
        pltpu.VMEM((6, 8, 256), jnp.int32),
        pltpu.SMEM((6, 8, 256), jnp.int32),
        pltpu.VMEM((1024, WIDTH), bf16), pltpu.VMEM((1024, WIDTH), bf16),
        pltpu.VMEM((6, *rows), f32),
        pltpu.VMEM((6, *rows), f32),
        pltpu.VMEM((6, *rows), f32),
        pltpu.VMEM((6, *rows), bf16),
        pltpu.VMEM((384, 1024), bf16), pltpu.VMEM((192, 1024), bf16),
        pltpu.VMEM((192, WIDTH), f32),
        pltpu.VMEM((192, WIDTH), bf16),
        pltpu.VMEM((192, WIDTH), bf16),
        dma((2, 2, 4)), dma((2, 3)), dma((2, 3)), dma((2, 8)), dma((2, 2, 8)), dma((2, 2, 8)), dma((2, 2)),
        dma((2,)), dma((3,)), dma, dma((4, 2, 3)), dma((2, 4)), dma((CHUNKS, 2)),
        dma((2, 8)), dma((2, 8)), dma((6,)), dma((6,)), dma((2, 2, 8)), dma((2, 2, 8)), dma((2, 2)), dma((2, 2)),
        dma((2,)), dma((3,)), dma, dma((3,)), dma, dma((CHUNKS, 2)), dma,
    ]
    any_space = pl.BlockSpec(memory_space=pl.ANY)
    vmem = pl.BlockSpec(memory_space=pltpu.VMEM)
    by_block = [a.reshape(PER_GROUP, BLK, GROUP) for a in (queries, keys, values)]
    return pl.pallas_call(
        kernel,
        out_shape=pltpu.VMEM((192, WIDTH), bf16),
        in_specs=[any_space, any_space, any_space, vmem, any_space],
        out_specs=vmem,
        scratch_shapes=scratch,
        compiler_params=pltpu.CompilerParams(
            collective_id=0, has_side_effects=True, vmem_limit_bytes=60 * 2**20
        ),
        name="attention",
    )(*by_block, block_mask, out_weight)


def solution(mesh):
    in_specs = (
        P("frame", "head"),
        P("frame", "head"),
        P("frame", "head"),
        P("frame", None),
        P("head", None),
    )
    out_specs = P(("frame", "head"), None)
    return jax.shard_map(
        per_device, mesh=mesh, in_specs=in_specs, out_specs=out_specs, check_vma=False
    )
```

```python
import math

import jax
import jax.numpy as jnp
from jax import lax
from jax.experimental import pallas as pl
from jax.experimental.pallas import tpu as pltpu
from jax.sharding import PartitionSpec as P

HEAD_DIM = 128
BLK = 128
GROUP = 768
PER_GROUP = GROUP // BLK
WIDTH = 3072
HEADS_CHIP = 12
PLANE = 8
CHUNK = 512
CHUNKS = WIDTH // CHUNK
EXP2_SCALE = HEAD_DIM ** (-0.5) * math.log2(math.e)
NEG = -1e30
MESH = pl.DeviceIdType.MESH


def live_blocks(mask):
    lane = lax.broadcasted_iota(jnp.int32, mask.shape, 1)
    at = lax.rem(lane, PER_GROUP)
    lanes = mask.shape[1]

    def ahead(value, by):
        return pltpu.roll(value, (lanes - by) % lanes, 1)

    before = jnp.where(at == 0, ahead(mask, PER_GROUP - 1), ahead(mask, lanes - 1))
    first = jnp.where((mask > 0) & (before == 0), at, 0)
    total = first
    for n in range(1, PER_GROUP):
        total = total + ahead(first, n)
    total = jnp.where((at == 0) & (lane < lanes - PER_GROUP), total, 0)
    shared = total
    for n in range(1, PER_GROUP):
        shared = shared + ahead(total, lanes - n)
    return lax.rem(shared + at, PER_GROUP)


def kernel(
    q_hbm, k_hbm, v_hbm, mask_hbm, w_hbm, out_ref,
    mask_ref, plane_a, plane_c, z_a, z_c, qbuf, blocks_ref, idx_v, idx_s, w_a, w_c, acc, top_s, sum_s, obuf, att_a, att_c,
    sums, sbuf, rbuf,
    kv_ss, q_ss, i_ss, pf_ss, z_ss, zf_ss, w_ss, wx_ss, wg_ss, wf_ss, o_ss, oc_ss, r_ss,
    p_rs, pf_rs, q_rs, i_rs, z_rs, zf_rs, w_rs, w_ls, wx_rs, wg_rs, wf_rs, a_rs, ac_rs, r_rs, s_sem,
):
    plane, zbuf, wbuf = (plane_a, plane_c), (z_a, z_c), (w_a, w_c)
    f = lax.axis_index("frame")
    h = lax.axis_index("head")
    z, yh, x = f // 8, lax.rem(f // 4, 2), lax.rem(f, 4)
    yl, c = h // 2, lax.rem(h, 2)
    g_me = lax.rem(f, 8)
    has_low, has_high = z > 0, z < 3

    def device(z_, g_, yl_, c_):
        return {"frame": z_ * 8 + g_, "head": yl_ * 2 + c_}

    other_core = device(z, g_me, yl, 1 - c)

    def remote(src, dst, ss, rs, target):
        return pltpu.make_async_remote_copy(
            src_ref=src, dst_ref=dst, send_sem=ss, recv_sem=rs, device_id=target, device_id_type=MESH
        )

    def is_me(target):
        return (target["frame"] == f) & (target["head"] == h)

    def send_or_copy(src, dst, ss, rs, target):
        mine = is_me(target)

        @pl.when(jnp.logical_not(mine))
        def _():
            remote(src, dst, ss, rs, target).start()

        @pl.when(mine)
        def _():
            pltpu.make_async_copy(src, dst, rs).start()

    def sent(src, dst, ss, rs, target):
        @pl.when(jnp.logical_not(is_me(target)))
        def _():
            remote(src, dst, ss, rs, target).wait_send()

    def arrived(ref, sem):
        pltpu.make_async_copy(ref, ref, sem).wait()

    load_mask = pltpu.make_async_copy(mask_hbm, mask_ref, s_sem)
    load_mask.start()

    barrier = pltpu.get_barrier_semaphore()

    def greet(target):
        pl.semaphore_signal(barrier, inc=1, device_id=target, device_id_type=MESH)

    dealer = x // 2

    def greet_plane(g, carry):
        greet(device(z, g, yl, jnp.where(g == g_me, 1 - c, dealer)))
        return carry

    lax.fori_loop(0, PLANE, greet_plane, 0)
    partner = [device(z, g_me, 1 - yl, c), device(z, (1 - yh) * 4 + x, 1 - yl, c)]
    for target in partner:
        greet(target)
    low, high = device(z - 1, g_me, yl, c), device(z + 1, g_me, yl, c)
    for n in (1, 3):
        greet(device(lax.rem(z + n, 4), g_me, yl, c))
    pl.semaphore_wait(barrier, jnp.where(dealer == c, 7, 9) + 2 + 2)

    e_me = x + yh * (3 - 2 * x)

    def kv_copies(hs):
        for n, (row, m) in enumerate(((0, 0), (0, 1), (1, 0), (1, 1))):
            to, i = lax.bitwise_xor(yh, row), lax.bitwise_xor(lax.rem(x, 2), m)
            at = pl.multiple_of((3 * i + (2 if hs else to)) * HEAD_DIM, HEAD_DIM)
            for t, src in enumerate((k_hbm, v_hbm)):
                yield (src.at[:, :, pl.ds(at, HEAD_DIM)], plane[hs].at[t, g_me],
                       kv_ss.at[t, hs, n], p_rs.at[hs, g_me], device(z, to * 4 + 2 * c + i, yl, t))

    def q_copies(hs):
        for i in range(2):
            for j in ((0, 1), (2,))[hs]:
                to, slot, core = (j, e_me, yh) if j < 2 else (yh, 4 + lax.rem(e_me, 2), e_me // 2)
                target = device(z, to * 4 + 2 * c + i, yl, core)
                yield blocks_ref, idx_v.at[slot], i_ss.at[i, j], i_rs.at[slot], target
                yield (q_hbm.at[:, :, pl.ds((3 * i + j) * HEAD_DIM, HEAD_DIM)], qbuf.at[slot],
                       q_ss.at[i, j], q_rs.at[slot], target)

    dealt = (lambda: kv_copies(0), lambda: q_copies(0), lambda: kv_copies(1), lambda: q_copies(1))
    for args in dealt[0]():
        send_or_copy(*args)
    load_mask.wait()
    blocks_ref[...] = jnp.zeros_like(blocks_ref)
    blocks_ref[:PER_GROUP, : mask_ref.shape[1]] = mask_ref[...]
    blocks_ref[...] = live_blocks(blocks_ref[...])
    for copies in dealt[1:]:
        for args in copies():
            send_or_copy(*args)

    def w_row(core, i, hs):
        return pl.multiple_of(yl * 512 + (2 * core + i) * 128 if hs else (2 * core + i) * 256, 128)

    def w_copies():
        for i in range(2):
            for hs, size in enumerate((256, 128)):
                yield (w_hbm.at[pl.ds(384 * i + 256 * hs, size), :],
                       wbuf[hs].at[pl.ds(w_row(c, i, hs), size), :], i, hs)

    for src, dst, i, hs in w_copies():
        pltpu.make_async_copy(src, dst, w_ls.at[i, hs]).start()

    def far_rows(core, part, size):
        return pl.ds(pl.multiple_of((1 - yl) * 512 + core * 256 + 64 * part, 64), size)

    def w_across(k):
        row = pl.multiple_of((x // 2) * 384 + 256 + 64 * lax.rem(x, 2) + 32 * k, 32)
        there = pl.ds(pl.multiple_of(yl * 512 + c * 256 + 64 * x + 32 * k, 32), 32)
        return remote(w_hbm.at[pl.ds(row, 32), :], w_c.at[there, :], wx_ss.at[k], wx_rs.at[k], partner[k])

    def w_round(n):
        here = w_c.at[far_rows(c, x, 64), :]
        x_to = lax.rem(x + n + 1, 4)
        return remote(here, here, wg_ss.at[n], wg_rs.at[n], device(z, yh * 4 + x_to, yl, c))

    def w_swap():
        here = w_c.at[far_rows(c, 0, 256), :]
        return remote(here, here, wf_ss, wf_rs, other_core)

    for k in range(2):
        w_across(k).start()

    def frame_of(step):
        return lax.bitwise_xor(step, g_me)

    def to_high(hs, g):
        return ((yh == 0) | (g // 4 == 1)) if hs else (g >= 0)

    def to_low(hs, g):
        return ((yh == 1) | (g // 4 == 0)) if hs else (g >= 0)

    def z_copy(way, hs, g):
        return remote(plane[hs].at[c, g], zbuf[hs].at[way, c, g], z_ss.at[way, hs, g], z_rs.at[way, hs, g],
                      (high, low)[way])

    def plane_forward(hs, g):
        return remote(plane[hs].at[c, g], plane[hs].at[c, g], pf_ss.at[hs, g], pf_rs.at[hs, g], other_core)

    def z_forward(way, hs, g):
        return remote(zbuf[hs].at[way, c, g], zbuf[hs].at[way, c, g], zf_ss.at[way, hs, g], zf_rs.at[way, hs, g],
                      other_core)

    def spread(hs, first, last):
        def one(step, carry):
            g = frame_of(step)
            arrived(plane[hs].at[c, g], p_rs.at[hs, g])

            @pl.when(has_high & to_high(hs, g))
            def _():
                z_copy(0, hs, g).start()

            @pl.when(has_low & to_low(hs, g))
            def _():
                z_copy(1, hs, g).start()

            plane_forward(hs, g).start()
            return carry

        lax.fori_loop(first, last, one, 0)

    def gets(way, hs, g):
        return (has_low & to_high(hs, g), has_high & to_low(hs, g))[way]

    def pass_on(hs, first, last):
        def one(step, carry):
            g = frame_of(step)
            for way in range(2):

                @pl.when(gets(way, hs, g))
                def _():
                    arrived(zbuf[hs].at[way, c, g], z_rs.at[way, hs, g])
                    z_forward(way, hs, g).start()

            return carry

        lax.fori_loop(first, last, one, 0)

    def other_plane(hs):
        def one(g, carry):
            arrived(plane[hs].at[1 - c, g], pf_rs.at[hs, g])
            return carry

        lax.fori_loop(0, PLANE, one, 0)

    def other_z(hs):
        def one(g, carry):
            for way in range(2):

                @pl.when(gets(way, hs, g))
                def _():
                    arrived(zbuf[hs].at[way, 1 - c, g], zf_rs.at[way, hs, g])

            return carry

        lax.fori_loop(0, PLANE, one, 0)

    side_of = (c, yh)

    def frame_at(e, side):
        return e + side * (7 - 2 * e)

    def scores_of(q, keys):
        return lax.dot_general(q, keys, (((1,), (1,)), ((), ())), preferred_element_type=jnp.float32)

    def rows_at(qb):
        return pl.ds(pl.multiple_of(qb * BLK, BLK), BLK)

    def block(u, qb, g, way, distance, j=0):
        group = jnp.clip(z * PLANE + g + (2 * way - 1) * distance, 0, 4 * PLANE - 1)
        return idx_s[u, qb, group * PER_GROUP + j]

    def plane_part(u, e, hs, out1, out2, qb):
        side = side_of[hs]
        g = frame_at(e, side)

        def near_block(by, j=0):
            way = 1 - side if by > 0 else side
            return frame_at(e + by, side), block(u, qb, g, way, abs(by), j)

        near = [near_block(1, j) for j in range(3)] + [near_block(2), near_block(4)]
        if out1:
            near += [near_block(-1, j) for j in range(3)]
        if out2:
            near += [near_block(-2)]
        q = qbuf[u, qb]

        def taken(t):
            return jnp.concatenate(
                [plane[hs][t, g].reshape(GROUP, HEAD_DIM)] + [plane[hs][t, gg, b] for gg, b in near], axis=0
            )

        keys, vals = taken(0), taken(1)
        s = scores_of(q, keys)
        top = jnp.max(s, axis=1, keepdims=True)
        p = jnp.exp2((s - top) * EXP2_SCALE)
        total = jnp.sum(p, axis=1, keepdims=True)
        acc[u, rows_at(qb), :] = jnp.dot(p.astype(jnp.bfloat16), vals, preferred_element_type=jnp.float32)
        top_s[u, rows_at(qb), :] = jnp.broadcast_to(top, (BLK, HEAD_DIM))
        sum_s[u, rows_at(qb), :] = jnp.broadcast_to(total, (BLK, HEAD_DIM))

    def z_part(u, e, hs, out1, out2, qb):
        side = side_of[hs]
        g = frame_at(e, side)

        def far_block(distance, j=0):
            return side, frame_at(e + PLANE - distance, side), block(u, qb, g, side, distance, j)

        far = [(way, g, block(u, qb, g, way, 8)) for way in range(2)] + [far_block(4)]
        if not out2:
            far += [far_block(2)]
        if not out1:
            far += [far_block(1, j) for j in range(3)]
        q = qbuf[u, qb]
        keys, vals, valid = [], [], []
        for way, gg, b in far:
            ok = ((way == 0) & has_low) | ((way == 1) & has_high)
            w2 = jnp.where(ok, way, 1 - way)
            g2 = jnp.where(ok, gg, g)
            keys.append(zbuf[hs][w2, 0, g2, b])
            vals.append(zbuf[hs][w2, 1, g2, b])
            valid.append(jnp.where(ok, 0.0, NEG))
        s = scores_of(q, jnp.concatenate(keys, axis=0))
        s = jnp.concatenate(
            [s[:, n * BLK : (n + 1) * BLK] + valid[n] for n in range(len(far))], axis=1
        )
        old = top_s[u, rows_at(qb), :]
        top = jnp.maximum(old[:, :1], jnp.max(s, axis=1, keepdims=True))
        p = jnp.exp2((s - top) * EXP2_SCALE)
        keep = jnp.exp2((old - top) * EXP2_SCALE)
        total = sum_s[u, rows_at(qb), :] * keep + jnp.sum(p, axis=1, keepdims=True)
        o = acc[u, rows_at(qb), :] * keep + jnp.dot(
            p.astype(jnp.bfloat16), jnp.concatenate(vals, axis=0), preferred_element_type=jnp.float32
        )
        obuf[u, rows_at(qb), :] = (o / total).astype(jnp.bfloat16)

    def query_blocks(first, last, unroll, part, *unit):
        def one(qb, carry):
            part(*unit, first + qb)
            return carry

        lax.fori_loop(0, last, one, 0, unroll=unroll)

    def own_o_copies(u):
        cols = pl.ds(pl.multiple_of((2 * x + yh) * HEAD_DIM, HEAD_DIM), HEAD_DIM)
        x_to = u + c * (3 - 2 * u)
        here, across = c * 4 + x_to, (1 - c) * 4 + x_to
        for t in range(2):
            mine, theirs = (2 * yl + t) * 192, (2 * (1 - yl) + t) * 192
            parts = ((mine, 192, 192, here), (theirs, 96, 0, here), (theirs + 96, 96, 96, across))
            for k, (row, size, at, to) in enumerate(parts):
                yield (obuf.at[u, pl.ds(pl.multiple_of(row, 96), size), :], att_a.at[pl.ds(at, size), cols],
                       o_ss.at[u, t, k], a_rs.at[k], device(z, to, yl, t))

    def shared_o_copies(u, e):
        cols = pl.ds(pl.multiple_of(yl * 512 + x * HEAD_DIM, HEAD_DIM), HEAD_DIM)
        to = yh * 4 + e + yh * (3 - 2 * e)
        for yl_to in range(2):
            for t in range(2):
                yield (obuf.at[u, pl.ds((2 * yl_to + t) * 192, 192), :], att_c.at[:, cols],
                       oc_ss.at[u - 4, 2 * yl_to + t], ac_rs, device(z, to, yl_to, t))

    own_kinds = (
        (1, lambda n: (0, 0), False, False),
        (1, lambda n: (1, 1), True, False),
        (2, lambda n: (2 + n, 2 + n), True, True),
    )
    shared_kinds = (
        (1 - c, lambda n: (4, 0), False, False),
        (1 - c, lambda n: (5, 1), True, False),
        (2 * c, lambda n: (4 + n, 2 + n), True, True),
    )

    def units_ready(first, last):
        for u in range(first, last):
            arrived(idx_v.at[u], i_rs.at[u])
        load = pltpu.make_async_copy(idx_v.at[pl.ds(first, last - first)], idx_s.at[pl.ds(first, last - first)], s_sem)
        load.start()
        load.wait()
        for u in range(first, last):
            arrived(qbuf.at[u], q_rs.at[u])

    spread(0, 0, PLANE)
    for src, dst, i, hs in w_copies():
        remote(src, dst, w_ss.at[i, hs], w_rs.at[i, hs], other_core).start()
    other_plane(0)
    units_ready(0, 4)
    for count, unit, out1, out2 in own_kinds:

        def own_plane(n, carry, unit=unit, out1=out1, out2=out2):
            u, e = unit(n)
            query_blocks(0, PER_GROUP, 3, plane_part, u, e, 0, out1, out2)
            spread(1, u, u + 1)
            pass_on(0, 2 * u, 2 * u + 2)
            return carry

        lax.fori_loop(0, count, own_plane, 0)
    other_z(0)
    for count, unit, out1, out2 in own_kinds:

        def own_far(n, carry, unit=unit, out1=out1, out2=out2):
            u, e = unit(n)
            query_blocks(0, PER_GROUP, 6, z_part, u, e, 0, out1, out2)
            for args in own_o_copies(u):
                send_or_copy(*args)
            return carry

        lax.fori_loop(0, count, own_far, 0)
    spread(1, 4, PLANE)
    pass_on(1, 0, 1)
    other_plane(1)
    units_ready(4, 6)
    for count, unit, out1, out2 in shared_kinds:

        def shared_plane(n, carry, unit=unit, out1=out1, out2=out2):
            u, e = unit(n)
            query_blocks(0, PER_GROUP, 3, plane_part, u, e, 1, out1, out2)
            pass_on(1, u - 3, u - 2)
            return carry

        lax.fori_loop(0, count, shared_plane, 0)

    for src, dst, i, hs in w_copies():
        pltpu.make_async_copy(src, dst, w_ls.at[i, hs]).wait()
    for i in range(2):
        for hs, size in enumerate((256, 128)):
            arrived(wbuf[hs].at[pl.ds(w_row(1 - c, i, hs), size), :], w_rs.at[i, hs])
    for k, (row, size) in enumerate(((192, 192), (0, 96), (96, 96))):
        arrived(att_a.at[pl.ds(row, size)], a_rs.at[k])

    def cols_at(n):
        return pl.ds(pl.multiple_of(n * CHUNK, CHUNK), CHUNK)

    def r_copy(n, k):
        rows = pl.ds(96 * k, 96)
        return remote(sbuf.at[rows, cols_at(n)], rbuf.at[rows, cols_at(n)], r_ss.at[n, k], r_rs.at[n, k], partner[k])

    def project_own(n, carry):
        r = jnp.dot(att_a[...], w_a[:, cols_at(n)], preferred_element_type=jnp.float32)
        sbuf[:, cols_at(n)] = r[:192].astype(jnp.bfloat16)
        sums[:, cols_at(n)] = r[192:]
        for k in range(2):
            r_copy(n, k).start()
        return carry

    def project_and_pass(n, carry):
        project_own(n, carry)
        pass_on(1, n + 3, n + 4)
        return carry

    for k in range(2):
        w_across(k).wait_recv()
    for n in range(3):
        w_round(n).start()
    lax.fori_loop(0, 5, project_and_pass, 0)
    lax.fori_loop(5, CHUNKS, project_own, 0)
    other_z(1)
    for count, unit, out1, out2 in shared_kinds:

        def shared_far(n, carry, unit=unit, out1=out1, out2=out2):
            u, e = unit(n)
            query_blocks(0, PER_GROUP, 6, z_part, u, e, 1, out1, out2)
            for args in shared_o_copies(u, e):
                send_or_copy(*args)
            return carry

        lax.fori_loop(0, count, shared_far, 0)

    def finish(n, carry):
        for k in range(2):
            r_copy(n, k).wait()
        total = sums[:, cols_at(n)] + rbuf[:, cols_at(n)].astype(jnp.float32)
        total = total + jnp.dot(att_c[...], w_c[:, cols_at(n)], preferred_element_type=jnp.float32)
        out_ref[:, cols_at(n)] = total.astype(jnp.bfloat16)
        return carry

    for n in range(3):
        arrived(w_c.at[far_rows(c, lax.rem(x + 3 - n, 4), 64), :], wg_rs.at[n])
    w_swap().start()
    for copies in dealt:
        for args in copies():
            sent(*args)
    for src, dst, i, hs in w_copies():
        remote(src, dst, w_ss.at[i, hs], w_rs.at[i, hs], other_core).wait_send()

    def done(g, carry):
        for hs in range(2):
            plane_forward(hs, g).wait_send()

            @pl.when(has_high & to_high(hs, g))
            def _():
                z_copy(0, hs, g).wait_send()

            @pl.when(has_low & to_low(hs, g))
            def _():
                z_copy(1, hs, g).wait_send()

            for way in range(2):

                @pl.when(gets(way, hs, g))
                def _():
                    z_forward(way, hs, g).wait_send()

        return carry

    lax.fori_loop(0, PLANE, done, 0)

    for k in range(2):
        w_across(k).wait_send()
    for n in range(3):
        w_round(n).wait_send()
    w_swap().wait_send()

    def own_done(u, carry):
        for args in own_o_copies(u):
            sent(*args)
        return carry

    lax.fori_loop(0, 4, own_done, 0)
    arrived(w_c.at[far_rows(1 - c, 0, 256), :], wf_rs)
    arrived(att_c, ac_rs)
    lax.fori_loop(0, CHUNKS, finish, 0)

    def shared_done(n, carry):
        for args in shared_o_copies(4 + n, 2 * c + n):
            sent(*args)
        return carry

    lax.fori_loop(0, 2, shared_done, 0)


def per_device(queries, keys, values, block_mask, out_weight):
    dma = pltpu.SemaphoreType.DMA
    bf16, f32 = jnp.bfloat16, jnp.float32
    rows, piece = (GROUP, HEAD_DIM), (PER_GROUP, BLK, HEAD_DIM)
    scratch = [
        pltpu.VMEM(block_mask.shape, jnp.int32),
        pltpu.VMEM((2, PLANE, *piece), bf16), pltpu.VMEM((2, PLANE, *piece), bf16),
        pltpu.VMEM((2, 2, PLANE, *piece), bf16), pltpu.VMEM((2, 2, PLANE, *piece), bf16),
        pltpu.VMEM((6, *piece), bf16),
        pltpu.VMEM((8, 256), jnp.int32),
        pltpu.VMEM((6, 8, 256), jnp.int32),
        pltpu.SMEM((6, 8, 256), jnp.int32),
        pltpu.VMEM((1024, WIDTH), bf16), pltpu.VMEM((1024, WIDTH), bf16),
        pltpu.VMEM((6, *rows), f32),
        pltpu.VMEM((6, *rows), f32),
        pltpu.VMEM((6, *rows), f32),
        pltpu.VMEM((6, *rows), bf16),
        pltpu.VMEM((384, 1024), bf16), pltpu.VMEM((192, 1024), bf16),
        pltpu.VMEM((192, WIDTH), f32),
        pltpu.VMEM((192, WIDTH), bf16),
        pltpu.VMEM((192, WIDTH), bf16),
        dma((2, 2, 4)), dma((2, 3)), dma((2, 3)), dma((2, 8)), dma((2, 2, 8)), dma((2, 2, 8)), dma((2, 2)),
        dma((2,)), dma((3,)), dma, dma((4, 2, 3)), dma((2, 4)), dma((CHUNKS, 2)),
        dma((2, 8)), dma((2, 8)), dma((6,)), dma((6,)), dma((2, 2, 8)), dma((2, 2, 8)), dma((2, 2)), dma((2, 2)),
        dma((2,)), dma((3,)), dma, dma((3,)), dma, dma((CHUNKS, 2)), dma,
    ]
    any_space = pl.BlockSpec(memory_space=pl.ANY)
    vmem = pl.BlockSpec(memory_space=pltpu.VMEM)
    by_block = [a.reshape(PER_GROUP, BLK, GROUP) for a in (queries, keys, values)]
    return pl.pallas_call(
        kernel,
        out_shape=pltpu.VMEM((192, WIDTH), bf16),
        in_specs=[any_space] * 5,
        out_specs=vmem,
        scratch_shapes=scratch,
        compiler_params=pltpu.CompilerParams(
            collective_id=0, has_side_effects=True, vmem_limit_bytes=60 * 2**20
        ),
        name="attention",
    )(*by_block, block_mask, out_weight)


def solution(mesh):
    in_specs = (
        P("frame", "head"),
        P("frame", "head"),
        P("frame", "head"),
        P("frame", None),
        P("head", None),
    )
    out_specs = P(("frame", "head"), None)
    return jax.shard_map(
        per_device, mesh=mesh, in_specs=in_specs, out_specs=out_specs, check_vma=False
    )
```

```python
import math

import jax
import jax.numpy as jnp
from jax import lax
from jax.experimental import pallas as pl
from jax.experimental.pallas import tpu as pltpu
from jax.sharding import PartitionSpec as P

HEAD_DIM = 128
BLK = 128
GROUP = 768
PER_GROUP = GROUP // BLK
WIDTH = 3072
HEADS_CHIP = 12
PLANE = 8
CHUNK = 512
CHUNKS = WIDTH // CHUNK
EXP2_SCALE = HEAD_DIM ** (-0.5) * math.log2(math.e)
NEG = -1e30
MESH = pl.DeviceIdType.MESH


def live_blocks(mask):
    lane = lax.broadcasted_iota(jnp.int32, mask.shape, 1)
    at = lax.rem(lane, PER_GROUP)
    lanes = mask.shape[1]

    def ahead(value, by):
        return pltpu.roll(value, (lanes - by) % lanes, 1)

    before = jnp.where(at == 0, ahead(mask, PER_GROUP - 1), ahead(mask, lanes - 1))
    first = jnp.where((mask > 0) & (before == 0), at, 0)
    total = first
    for n in range(1, PER_GROUP):
        total = total + ahead(first, n)
    total = jnp.where((at == 0) & (lane < lanes - PER_GROUP), total, 0)
    shared = total
    for n in range(1, PER_GROUP):
        shared = shared + ahead(total, lanes - n)
    return lax.rem(shared + at, PER_GROUP)


def kernel(
    q_hbm, k_hbm, v_hbm, mask_hbm, w_hbm, out_ref,
    mask_ref, plane_a, plane_c, z_a, z_c, qbuf, blocks_ref, idx_v, idx_s, w_a, w_c, acc, top_s, sum_s, obuf, att_a, att_c,
    sums, sbuf, rbuf,
    kv_ss, q_ss, i_ss, pf_ss, z_ss, zf_ss, w_ss, wx_ss, wg_ss, wf_ss, o_ss, oc_ss, r_ss,
    p_rs, pf_rs, q_rs, i_rs, z_rs, zf_rs, w_rs, w_ls, wx_rs, wg_rs, wf_rs, a_rs, ac_rs, r_rs, s_sem,
):
    plane, zbuf, wbuf = (plane_a, plane_c), (z_a, z_c), (w_a, w_c)
    f = lax.axis_index("frame")
    h = lax.axis_index("head")
    z, yh, x = f // 8, lax.rem(f // 4, 2), lax.rem(f, 4)
    yl, c = h // 2, lax.rem(h, 2)
    g_me = lax.rem(f, 8)
    has_low, has_high = z > 0, z < 3

    def device(z_, g_, yl_, c_):
        return {"frame": z_ * 8 + g_, "head": yl_ * 2 + c_}

    other_core = device(z, g_me, yl, 1 - c)

    def remote(src, dst, ss, rs, target):
        return pltpu.make_async_remote_copy(
            src_ref=src, dst_ref=dst, send_sem=ss, recv_sem=rs, device_id=target, device_id_type=MESH
        )

    def is_me(target):
        return (target["frame"] == f) & (target["head"] == h)

    def send_or_copy(src, dst, ss, rs, target):
        mine = is_me(target)

        @pl.when(jnp.logical_not(mine))
        def _():
            remote(src, dst, ss, rs, target).start()

        @pl.when(mine)
        def _():
            pltpu.make_async_copy(src, dst, rs).start()

    def sent(src, dst, ss, rs, target):
        @pl.when(jnp.logical_not(is_me(target)))
        def _():
            remote(src, dst, ss, rs, target).wait_send()

    def arrived(ref, sem):
        pltpu.make_async_copy(ref, ref, sem).wait()

    load_mask = pltpu.make_async_copy(mask_hbm, mask_ref, s_sem)
    load_mask.start()

    barrier = pltpu.get_barrier_semaphore()

    def greet(target):
        pl.semaphore_signal(barrier, inc=1, device_id=target, device_id_type=MESH)

    dealer = x // 2

    def greet_plane(g, carry):
        greet(device(z, g, yl, jnp.where(g == g_me, 1 - c, dealer)))
        return carry

    lax.fori_loop(0, PLANE, greet_plane, 0)
    partner = [device(z, g_me, 1 - yl, c), device(z, (1 - yh) * 4 + x, 1 - yl, c)]
    for target in partner:
        greet(target)
    low, high = device(z - 1, g_me, yl, c), device(z + 1, g_me, yl, c)
    for n in (1, 3):
        greet(device(lax.rem(z + n, 4), g_me, yl, c))
    pl.semaphore_wait(barrier, jnp.where(dealer == c, 7, 9) + 2 + 2)

    e_me = x + yh * (3 - 2 * x)

    def kv_copies(hs):
        for n, (row, m) in enumerate(((0, 0), (0, 1), (1, 0), (1, 1))):
            to, i = lax.bitwise_xor(yh, row), lax.bitwise_xor(lax.rem(x, 2), m)
            at = pl.multiple_of((3 * i + (2 if hs else to)) * HEAD_DIM, HEAD_DIM)
            for t, src in enumerate((k_hbm, v_hbm)):
                yield (src.at[:, :, pl.ds(at, HEAD_DIM)], plane[hs].at[t, g_me],
                       kv_ss.at[t, hs, n], p_rs.at[hs, g_me], device(z, to * 4 + 2 * c + i, yl, t))

    def q_copies(hs):
        for i in range(2):
            for j in ((0, 1), (2,))[hs]:
                to, slot, core = (j, e_me, yh) if j < 2 else (yh, 4 + e_me // 2, lax.rem(e_me, 2))
                target = device(z, to * 4 + 2 * c + i, yl, core)
                yield blocks_ref, idx_v.at[slot], i_ss.at[i, j], i_rs.at[slot], target
                yield (q_hbm.at[:, :, pl.ds((3 * i + j) * HEAD_DIM, HEAD_DIM)], qbuf.at[slot],
                       q_ss.at[i, j], q_rs.at[slot], target)

    dealt = (lambda: kv_copies(0), lambda: q_copies(0), lambda: kv_copies(1), lambda: q_copies(1))
    for args in dealt[0]():
        send_or_copy(*args)
    load_mask.wait()
    blocks_ref[...] = jnp.zeros_like(blocks_ref)
    blocks_ref[:PER_GROUP, : mask_ref.shape[1]] = mask_ref[...]
    blocks_ref[...] = live_blocks(blocks_ref[...])
    for copies in dealt[1:]:
        for args in copies():
            send_or_copy(*args)

    def w_row(core, i, hs):
        return pl.multiple_of(yl * 512 + (2 * core + i) * 128 if hs else (2 * core + i) * 256, 128)

    def w_copies():
        for i in range(2):
            for hs, size in enumerate((256, 128)):
                yield (w_hbm.at[pl.ds(384 * i + 256 * hs, size), :],
                       wbuf[hs].at[pl.ds(w_row(c, i, hs), size), :], i, hs)

    for src, dst, i, hs in w_copies():
        pltpu.make_async_copy(src, dst, w_ls.at[i, hs]).start()

    def far_rows(core, part, size):
        return pl.ds(pl.multiple_of((1 - yl) * 512 + core * 256 + 64 * part, 64), size)

    def w_across(k):
        row = pl.multiple_of((x // 2) * 384 + 256 + 64 * lax.rem(x, 2) + 32 * k, 32)
        there = pl.ds(pl.multiple_of(yl * 512 + c * 256 + 64 * x + 32 * k, 32), 32)
        return remote(w_hbm.at[pl.ds(row, 32), :], w_c.at[there, :], wx_ss.at[k], wx_rs.at[k], partner[k])

    def w_round(n):
        here = w_c.at[far_rows(c, x, 64), :]
        x_to = lax.rem(x + n + 1, 4)
        return remote(here, here, wg_ss.at[n], wg_rs.at[n], device(z, yh * 4 + x_to, yl, c))

    def w_swap():
        here = w_c.at[far_rows(c, 0, 256), :]
        return remote(here, here, wf_ss, wf_rs, other_core)

    for k in range(2):
        w_across(k).start()

    def frame_of(step):
        return lax.bitwise_xor(step, g_me)

    def to_high(hs, g):
        return ((yh == 0) | (g // 4 == 1)) if hs else (g >= 0)

    def to_low(hs, g):
        return ((yh == 1) | (g // 4 == 0)) if hs else (g >= 0)

    def z_copy(way, hs, g):
        return remote(plane[hs].at[c, g], zbuf[hs].at[way, c, g], z_ss.at[way, hs, g], z_rs.at[way, hs, g],
                      (high, low)[way])

    def plane_forward(hs, g):
        return remote(plane[hs].at[c, g], plane[hs].at[c, g], pf_ss.at[hs, g], pf_rs.at[hs, g], other_core)

    def z_forward(way, hs, g):
        return remote(zbuf[hs].at[way, c, g], zbuf[hs].at[way, c, g], zf_ss.at[way, hs, g], zf_rs.at[way, hs, g],
                      other_core)

    def spread(hs, first, last):
        def one(step, carry):
            g = frame_of(step)
            arrived(plane[hs].at[c, g], p_rs.at[hs, g])

            @pl.when(has_high & to_high(hs, g))
            def _():
                z_copy(0, hs, g).start()

            @pl.when(has_low & to_low(hs, g))
            def _():
                z_copy(1, hs, g).start()

            plane_forward(hs, g).start()
            return carry

        lax.fori_loop(first, last, one, 0)

    def gets(way, hs, g):
        return (has_low & to_high(hs, g), has_high & to_low(hs, g))[way]

    def pass_on(hs, first, last):
        def one(step, carry):
            g = frame_of(step)
            for way in range(2):

                @pl.when(gets(way, hs, g))
                def _():
                    arrived(zbuf[hs].at[way, c, g], z_rs.at[way, hs, g])
                    z_forward(way, hs, g).start()

            return carry

        lax.fori_loop(first, last, one, 0)

    def other_plane(hs):
        def one(g, carry):
            arrived(plane[hs].at[1 - c, g], pf_rs.at[hs, g])
            return carry

        lax.fori_loop(0, PLANE, one, 0)

    def other_z(hs):
        def one(g, carry):
            for way in range(2):

                @pl.when(gets(way, hs, g))
                def _():
                    arrived(zbuf[hs].at[way, 1 - c, g], zf_rs.at[way, hs, g])

            return carry

        lax.fori_loop(0, PLANE, one, 0)

    side_of = (c, yh)

    def frame_at(e, side):
        return e + side * (7 - 2 * e)

    def scores_of(q, keys):
        return lax.dot_general(q, keys, (((1,), (1,)), ((), ())), preferred_element_type=jnp.float32)

    def rows_at(qb):
        return pl.ds(pl.multiple_of(qb * BLK, BLK), BLK)

    def block(u, qb, g, way, distance, j=0):
        group = jnp.clip(z * PLANE + g + (2 * way - 1) * distance, 0, 4 * PLANE - 1)
        return idx_s[u, qb, group * PER_GROUP + j]

    def plane_part(u, e, hs, out1, out2, qb):
        side = side_of[hs]
        g = frame_at(e, side)

        def near_block(by, j=0):
            way = 1 - side if by > 0 else side
            return frame_at(e + by, side), block(u, qb, g, way, abs(by), j)

        near = [near_block(1, j) for j in range(3)] + [near_block(2), near_block(4)]
        if out1:
            near += [near_block(-1, j) for j in range(3)]
        if out2:
            near += [near_block(-2)]
        q = qbuf[u, qb]

        def taken(t):
            return jnp.concatenate(
                [plane[hs][t, g].reshape(GROUP, HEAD_DIM)] + [plane[hs][t, gg, b] for gg, b in near], axis=0
            )

        keys, vals = taken(0), taken(1)
        s = scores_of(q, keys)
        top = jnp.max(s, axis=1, keepdims=True)
        p = jnp.exp2((s - top) * EXP2_SCALE)
        total = jnp.sum(p, axis=1, keepdims=True)
        acc[u, rows_at(qb), :] = jnp.dot(p.astype(jnp.bfloat16), vals, preferred_element_type=jnp.float32)
        top_s[u, rows_at(qb), :] = jnp.broadcast_to(top, (BLK, HEAD_DIM))
        sum_s[u, rows_at(qb), :] = jnp.broadcast_to(total, (BLK, HEAD_DIM))

    def z_part(u, e, hs, out1, out2, qb):
        side = side_of[hs]
        g = frame_at(e, side)

        def far_block(distance, j=0):
            return side, frame_at(e + PLANE - distance, side), block(u, qb, g, side, distance, j)

        far = [(way, g, block(u, qb, g, way, 8)) for way in range(2)] + [far_block(4)]
        if not out2:
            far += [far_block(2)]
        if not out1:
            far += [far_block(1, j) for j in range(3)]
        q = qbuf[u, qb]
        keys, vals, valid = [], [], []
        for way, gg, b in far:
            ok = ((way == 0) & has_low) | ((way == 1) & has_high)
            w2 = jnp.where(ok, way, 1 - way)
            g2 = jnp.where(ok, gg, g)
            keys.append(zbuf[hs][w2, 0, g2, b])
            vals.append(zbuf[hs][w2, 1, g2, b])
            valid.append(jnp.where(ok, 0.0, NEG))
        s = scores_of(q, jnp.concatenate(keys, axis=0))
        s = jnp.concatenate(
            [s[:, n * BLK : (n + 1) * BLK] + valid[n] for n in range(len(far))], axis=1
        )
        old = top_s[u, rows_at(qb), :]
        top = jnp.maximum(old[:, :1], jnp.max(s, axis=1, keepdims=True))
        p = jnp.exp2((s - top) * EXP2_SCALE)
        keep = jnp.exp2((old - top) * EXP2_SCALE)
        total = sum_s[u, rows_at(qb), :] * keep + jnp.sum(p, axis=1, keepdims=True)
        o = acc[u, rows_at(qb), :] * keep + jnp.dot(
            p.astype(jnp.bfloat16), jnp.concatenate(vals, axis=0), preferred_element_type=jnp.float32
        )
        obuf[u, rows_at(qb), :] = (o / total).astype(jnp.bfloat16)

    def query_blocks(first, last, unroll, part, *unit):
        def one(qb, carry):
            part(*unit, first + qb)
            return carry

        lax.fori_loop(0, last, one, 0, unroll=unroll)

    def own_o_copies(u):
        cols = pl.ds(pl.multiple_of((2 * x + yh) * HEAD_DIM, HEAD_DIM), HEAD_DIM)
        x_to = u + c * (3 - 2 * u)
        here, across = c * 4 + x_to, (1 - c) * 4 + x_to
        for t in range(2):
            mine, theirs = (2 * yl + t) * 192, (2 * (1 - yl) + t) * 192
            parts = ((mine, 192, 192, here), (theirs, 96, 0, here), (theirs + 96, 96, 96, across))
            for k, (row, size, at, to) in enumerate(parts):
                yield (obuf.at[u, pl.ds(pl.multiple_of(row, 96), size), :], att_a.at[pl.ds(at, size), cols],
                       o_ss.at[u, t, k], a_rs.at[k], device(z, to, yl, t))

    def shared_o_copies(u, e):
        cols = pl.ds(pl.multiple_of(yl * 512 + x * HEAD_DIM, HEAD_DIM), HEAD_DIM)
        to = yh * 4 + e + yh * (3 - 2 * e)
        for yl_to in range(2):
            for t in range(2):
                yield (obuf.at[u, pl.ds((2 * yl_to + t) * 192, 192), :], att_c.at[:, cols],
                       oc_ss.at[u - 4, 2 * yl_to + t], ac_rs, device(z, to, yl_to, t))

    own_kinds = (
        (1, lambda n: (0, 0), False, False),
        (1, lambda n: (1, 1), True, False),
        (2, lambda n: (2 + n, 2 + n), True, True),
    )
    shared_kinds = (
        (1 - c, lambda n: (4, 0), False, False),
        (c, lambda n: (4, 1), True, False),
        (1, lambda n: (5, 2 + c), True, True),
    )

    def units_ready(first, last):
        for u in range(first, last):
            arrived(idx_v.at[u], i_rs.at[u])
        load = pltpu.make_async_copy(idx_v.at[pl.ds(first, last - first)], idx_s.at[pl.ds(first, last - first)], s_sem)
        load.start()
        load.wait()
        for u in range(first, last):
            arrived(qbuf.at[u], q_rs.at[u])

    spread(0, 0, PLANE)
    for src, dst, i, hs in w_copies():
        remote(src, dst, w_ss.at[i, hs], w_rs.at[i, hs], other_core).start()
    other_plane(0)
    units_ready(0, 4)
    for count, unit, out1, out2 in own_kinds:

        def own_plane(n, carry, unit=unit, out1=out1, out2=out2):
            u, e = unit(n)
            query_blocks(0, PER_GROUP, 3, plane_part, u, e, 0, out1, out2)
            spread(1, u, u + 1)
            pass_on(0, 2 * u, 2 * u + 2)
            return carry

        lax.fori_loop(0, count, own_plane, 0)
    other_z(0)
    for count, unit, out1, out2 in own_kinds:

        def own_far(n, carry, unit=unit, out1=out1, out2=out2):
            u, e = unit(n)
            query_blocks(0, PER_GROUP, 6, z_part, u, e, 0, out1, out2)
            for args in own_o_copies(u):
                send_or_copy(*args)
            return carry

        lax.fori_loop(0, count, own_far, 0)
    spread(1, 4, PLANE)
    pass_on(1, 0, 1)
    other_plane(1)
    units_ready(4, 6)
    for count, unit, out1, out2 in shared_kinds:

        def shared_plane(n, carry, unit=unit, out1=out1, out2=out2):
            u, e = unit(n)
            query_blocks(0, PER_GROUP, 3, plane_part, u, e, 1, out1, out2)
            pass_on(1, u - 3, u - 2)
            return carry

        lax.fori_loop(0, count, shared_plane, 0)

    for src, dst, i, hs in w_copies():
        pltpu.make_async_copy(src, dst, w_ls.at[i, hs]).wait()
    for i in range(2):
        for hs, size in enumerate((256, 128)):
            arrived(wbuf[hs].at[pl.ds(w_row(1 - c, i, hs), size), :], w_rs.at[i, hs])
    for k, (row, size) in enumerate(((192, 192), (0, 96), (96, 96))):
        arrived(att_a.at[pl.ds(row, size)], a_rs.at[k])

    def cols_at(n):
        return pl.ds(pl.multiple_of(n * CHUNK, CHUNK), CHUNK)

    def r_copy(n, k):
        rows = pl.ds(96 * k, 96)
        return remote(sbuf.at[rows, cols_at(n)], rbuf.at[rows, cols_at(n)], r_ss.at[n, k], r_rs.at[n, k], partner[k])

    def project_own(n, carry):
        r = jnp.dot(att_a[...], w_a[:, cols_at(n)], preferred_element_type=jnp.float32)
        sbuf[:, cols_at(n)] = r[:192].astype(jnp.bfloat16)
        sums[:, cols_at(n)] = r[192:]
        for k in range(2):
            r_copy(n, k).start()
        return carry

    def project_and_pass(n, carry):
        project_own(n, carry)
        pass_on(1, n + 3, n + 4)
        return carry

    for k in range(2):
        w_across(k).wait_recv()
    for n in range(3):
        w_round(n).start()
    lax.fori_loop(0, 5, project_and_pass, 0)
    lax.fori_loop(5, CHUNKS, project_own, 0)
    other_z(1)
    for count, unit, out1, out2 in shared_kinds:

        def shared_far(n, carry, unit=unit, out1=out1, out2=out2):
            u, e = unit(n)
            query_blocks(0, PER_GROUP, 6, z_part, u, e, 1, out1, out2)
            for args in shared_o_copies(u, e):
                send_or_copy(*args)
            return carry

        lax.fori_loop(0, count, shared_far, 0)

    def finish(n, carry):
        for k in range(2):
            r_copy(n, k).wait()
        total = sums[:, cols_at(n)] + rbuf[:, cols_at(n)].astype(jnp.float32)
        total = total + jnp.dot(att_c[...], w_c[:, cols_at(n)], preferred_element_type=jnp.float32)
        out_ref[:, cols_at(n)] = total.astype(jnp.bfloat16)
        return carry

    for n in range(3):
        arrived(w_c.at[far_rows(c, lax.rem(x + 3 - n, 4), 64), :], wg_rs.at[n])
    w_swap().start()
    for copies in dealt:
        for args in copies():
            sent(*args)
    for src, dst, i, hs in w_copies():
        remote(src, dst, w_ss.at[i, hs], w_rs.at[i, hs], other_core).wait_send()

    def done(g, carry):
        for hs in range(2):
            plane_forward(hs, g).wait_send()

            @pl.when(has_high & to_high(hs, g))
            def _():
                z_copy(0, hs, g).wait_send()

            @pl.when(has_low & to_low(hs, g))
            def _():
                z_copy(1, hs, g).wait_send()

            for way in range(2):

                @pl.when(gets(way, hs, g))
                def _():
                    z_forward(way, hs, g).wait_send()

        return carry

    lax.fori_loop(0, PLANE, done, 0)

    for k in range(2):
        w_across(k).wait_send()
    for n in range(3):
        w_round(n).wait_send()
    w_swap().wait_send()

    def own_done(u, carry):
        for args in own_o_copies(u):
            sent(*args)
        return carry

    lax.fori_loop(0, 4, own_done, 0)
    arrived(w_c.at[far_rows(1 - c, 0, 256), :], wf_rs)
    arrived(att_c, ac_rs)
    lax.fori_loop(0, CHUNKS, finish, 0)

    def shared_done(n, carry):
        for args in shared_o_copies(4 + n, c + 2 * n):
            sent(*args)
        return carry

    lax.fori_loop(0, 2, shared_done, 0)


def per_device(queries, keys, values, block_mask, out_weight):
    dma = pltpu.SemaphoreType.DMA
    bf16, f32 = jnp.bfloat16, jnp.float32
    rows, piece = (GROUP, HEAD_DIM), (PER_GROUP, BLK, HEAD_DIM)
    scratch = [
        pltpu.VMEM(block_mask.shape, jnp.int32),
        pltpu.VMEM((2, PLANE, *piece), bf16), pltpu.VMEM((2, PLANE, *piece), bf16),
        pltpu.VMEM((2, 2, PLANE, *piece), bf16), pltpu.VMEM((2, 2, PLANE, *piece), bf16),
        pltpu.VMEM((6, *piece), bf16),
        pltpu.VMEM((8, 256), jnp.int32),
        pltpu.VMEM((6, 8, 256), jnp.int32),
        pltpu.SMEM((6, 8, 256), jnp.int32),
        pltpu.VMEM((1024, WIDTH), bf16), pltpu.VMEM((1024, WIDTH), bf16),
        pltpu.VMEM((6, *rows), f32),
        pltpu.VMEM((6, *rows), f32),
        pltpu.VMEM((6, *rows), f32),
        pltpu.VMEM((6, *rows), bf16),
        pltpu.VMEM((384, 1024), bf16), pltpu.VMEM((192, 1024), bf16),
        pltpu.VMEM((192, WIDTH), f32),
        pltpu.VMEM((192, WIDTH), bf16),
        pltpu.VMEM((192, WIDTH), bf16),
        dma((2, 2, 4)), dma((2, 3)), dma((2, 3)), dma((2, 8)), dma((2, 2, 8)), dma((2, 2, 8)), dma((2, 2)),
        dma((2,)), dma((3,)), dma, dma((4, 2, 3)), dma((2, 4)), dma((CHUNKS, 2)),
        dma((2, 8)), dma((2, 8)), dma((6,)), dma((6,)), dma((2, 2, 8)), dma((2, 2, 8)), dma((2, 2)), dma((2, 2)),
        dma((2,)), dma((3,)), dma, dma((3,)), dma, dma((CHUNKS, 2)), dma,
    ]
    any_space = pl.BlockSpec(memory_space=pl.ANY)
    vmem = pl.BlockSpec(memory_space=pltpu.VMEM)
    by_block = [a.reshape(PER_GROUP, BLK, GROUP) for a in (queries, keys, values)]
    return pl.pallas_call(
        kernel,
        out_shape=pltpu.VMEM((192, WIDTH), bf16),
        in_specs=[any_space] * 5,
        out_specs=vmem,
        scratch_shapes=scratch,
        compiler_params=pltpu.CompilerParams(
            collective_id=0, has_side_effects=True, vmem_limit_bytes=60 * 2**20
        ),
        name="attention",
    )(*by_block, block_mask, out_weight)


def solution(mesh):
    in_specs = (
        P("frame", "head"),
        P("frame", "head"),
        P("frame", "head"),
        P("frame", None),
        P("head", None),
    )
    out_specs = P(("frame", "head"), None)
    return jax.shard_map(
        per_device, mesh=mesh, in_specs=in_specs, out_specs=out_specs, check_vma=False
    )
```
